256 devices in a mesh: expert: 16 (over x, z_lo, core), split: 16 (over z_hi, y).
Axes of the slice: x: 4, y: 4, z: 8 (z_hi: 4, z_lo: 2; z = z_hi * 2 + z_lo), core: 2. Of those that a mesh axis runs over, the one named last changes fastest.
Arguments:
- tokens: bfloat16 [4096, 3072], P('expert', 'split'), may hold values from -6 to 6
- expert_ids: int32 [4096, 2], P('expert'), may hold values from 0 to 15, all different within a row; in each aligned block of 256 rows (0 to 255, 256 to 511, ...) at most 64 rows name the same one
- pair_logits: float32 [4096, 2], P('expert'), may hold values from -6 to 6
- gate_weight: bfloat16 [16, 3072, 8192], P('expert', None, 'split'), may hold values from -0.109375 to 0.109375
- up_weight: bfloat16 [16, 3072, 8192], P('expert', None, 'split'), may hold values from -0.109375 to 0.109375
- down_weight: bfloat16 [16, 8192, 3072], P('expert', 'split'), may hold values from -0.0625 to 0.0625
Outputs:
- mixed: bfloat16 [4096, 3072], P('expert', 'split')
The draws below stay inside these ranges and needn't reach their ends.
Inputs may be any that keep to these rules, and one draw needn't show every extreme that they name: `expert_ids`: the two experts of a token differ. Within each aligned block of 256 tokens (the tokens of one index of expert) no expert is named by more than 64 pairs, a bound that some block reaches.
All inputs are finite; a program needn't handle non-finite values.
Results may differ from the reference program's by a relative error of at most 0.019.
Values may be sent and summed in bfloat16 or wider, within the bound.
A program may use at most 64 MiB of HBM per device.

```python
import math
import jax
import jax.numpy as jnp
import numpy as np
from jax import lax

D = 3072
FF = 8192
TOK_E = 256
EXPERTS = 16
CAP = 64
TOKENS = 4096
N_EXPERT = 16
N_SPLIT = 16


def levels(rng, dims, cuts, least, largest):
    def one(dim, blocks):
        steps = jax.random.uniform(jax.random.fold_in(jax.random.fold_in(rng, 6), dim), (blocks,), jnp.float32, least / len(cuts), largest / len(cuts))
        return jnp.repeat(jnp.exp(steps), dims[dim] // blocks).reshape((-1,) + (1,) * (len(dims) - dim - 1))

    factor_of = one(*cuts[0])
    for cut in cuts[1:]:
        factor_of = factor_of * one(*cut)
    return factor_of


def shared_out(key, own, number, rows, number_of, top, bound, skew):
    order = jax.random.permutation(key, number_of)
    heavy_load, common = load_shares(number_of, rows * top, bound, skew, True), load_shares(number_of, rows * top, bound, skew, False)
    places = jnp.arange(number_of)

    def named(lengths, offset_by):
        used = int((lengths > 0).sum())
        fixed = max(1, used // 4)
        shifted = fixed + (places - fixed + offset_by * (used - fixed)) % max(1, number_of - fixed)
        return jnp.zeros((number_of,), jnp.int32).at[order[jnp.where(places < fixed, places, shifted)]].set(jnp.asarray(lengths, jnp.int32))

    lengths = jnp.where(number % 4 == 0, named(heavy_load, number // 4), named(common, number - number // 4 - 1))
    mixed = jax.random.permutation(jax.random.fold_in(own, 3), number_of)
    giver, receiver = mixed[0:number_of // 2 * 2:2], mixed[1:number_of // 2 * 2:2]
    slack = jnp.minimum(lengths[giver] - 1, bound - lengths[receiver]) // 2
    slack = jnp.where((giver == order[0]) | (receiver == order[0]) | (lengths[receiver] == 0), 0, jnp.maximum(slack, 0))
    shifted = jax.random.randint(jax.random.fold_in(own, 4), (number_of // 2,), 0, 1 << 20) % (slack + 1)
    lengths = lengths.at[giver].add(-shifted).at[receiver].add(shifted)
    members = jnp.searchsorted(jnp.cumsum(lengths), jnp.arange(rows * top), side="right").astype(jnp.int32)
    table = members.reshape(top, rows).T
    table = table[jax.random.permutation(jax.random.fold_in(own, 1), rows)]
    offset_by = jax.random.randint(jax.random.fold_in(own, 2), (rows, 1), 0, top)
    return jnp.take_along_axis(table, (jnp.arange(top)[None, :] + offset_by) % top, axis=1)


def load_shares(amount, total, limit, lean, full):
    weights = [(1 << 20) // math.isqrt(rank ** lean) + 1 for rank in range(1, amount + 1)]
    largest = limit if full else min(limit, max(-(-total // amount), total * weights[0] // sum(weights)))
    least = 1 if total - largest >= amount - 1 else 0
    counts, surplus = [largest] + [least] * (amount - 1), total - largest - least * (amount - 1)
    while surplus > 0:
        movable = [i for i in range(1, amount) if counts[i] < largest] or [i for i in range(1, amount) if counts[i] < limit]
        whole, budget = sum([weights[i] for i in movable]), surplus
        for i in movable:
            extra = min(limit - counts[i], max(1, budget * weights[i] // whole), surplus)
            counts[i] = counts[i] + extra
            surplus = surplus - extra
    return np.array(counts)


def noise(rng, shape, scale, limit, split=(), kind=jnp.bfloat16):
    entries = jax.random.normal(rng, shape, jnp.float32) * scale
    if len(split) > 0:
        entries = levels(rng, shape, split, -0.22, 0.18) * entries
    return jnp.clip(entries, min=-limit, max=limit).astype(kind)


def setup_inputs(seed: int = 0) -> dict:
    splits = jax.random.split(jax.random.key(seed), 7)
    tokens = noise(splits[0], (TOKENS, D), 1.0, 6.0, ((0, 16), (1, 16)))
    expert_ids_keys = jax.random.split(jax.random.fold_in(splits[1], 1), TOKENS // TOK_E)
    expert_ids_turns = jax.random.permutation(jax.random.fold_in(splits[1], 3), TOKENS // TOK_E)
    expert_ids = jax.vmap(lambda own, number: shared_out(jax.random.fold_in(splits[1], 2), own, number, TOK_E, EXPERTS, 2, CAP, 2))(expert_ids_keys, expert_ids_turns).reshape((TOKENS, 2))
    pair_logits = noise(splits[2], (TOKENS, 2), 1.5, 6.0, ((0, 16),), jnp.float32)
    gate_weight = noise(splits[3], (EXPERTS, D, FF), D ** -0.5, 0.109375, ((0, 16), (2, 16)))
    up_weight = noise(splits[4], (EXPERTS, D, FF), D ** -0.5, 0.109375, ((0, 16), (2, 16)))
    down_weight = noise(splits[5], (EXPERTS, FF, D), FF ** -0.5, 0.0625, ((0, 16), (1, 16)))
    return {"tokens": tokens, "expert_ids": expert_ids, "pair_logits": pair_logits, "gate_weight": gate_weight, "up_weight": up_weight, "down_weight": down_weight}


def reference(tokens, expert_ids, pair_logits, gate_weight, up_weight, down_weight):
    first = jax.nn.sigmoid(pair_logits[:, 0] - pair_logits[:, 1])
    mix = jnp.stack([first, 1.0 - first], axis=1).reshape(-1)
    flat = expert_ids.reshape(-1).astype(jnp.int32)
    blocks = flat.reshape(N_EXPERT, 2 * TOK_E)
    labels = jnp.arange(EXPERTS, dtype=jnp.int32)
    onehot = (blocks[:, :, None] == labels[None, None, :]).astype(jnp.int32)
    before = jnp.cumsum(onehot, axis=1) - onehot
    slot = jnp.sum(before * onehot, axis=2).reshape(-1).astype(jnp.int32)
    pair_block = (jnp.arange(2 * TOKENS, dtype=jnp.int32) // (2 * TOK_E)).astype(jnp.int32)
    dest = (pair_block * CAP + slot).astype(jnp.int32)
    count = N_EXPERT * CAP
    doubled = jnp.repeat(tokens, 2, axis=0)
    group = FF // N_SPLIT

    def one_expert(total, index):
        hit = flat == index
        target = jnp.where(hit, dest, count).astype(jnp.int32)
        rows = jnp.zeros((count + 1, D), tokens.dtype).at[target].set(doubled)[:count]
        gate = jnp.dot(rows, gate_weight[index], preferred_element_type=jnp.float32)
        up = jnp.dot(rows, up_weight[index], preferred_element_type=jnp.float32)
        hidden = (jax.nn.silu(gate) * up).astype(jnp.bfloat16)
        hid = hidden.reshape(count, N_SPLIT, group).astype(jnp.float32)
        down = down_weight[index].reshape(N_SPLIT, group, D).astype(jnp.float32)
        parts = jnp.einsum("rsf,sfd->srd", hid, down).astype(jnp.bfloat16)
        parts = lax.optimization_barrier(parts).astype(jnp.float32)
        result = jnp.sum(parts, axis=0)
        picked = result[jnp.minimum(target, count - 1)]
        weight = jnp.where(hit, mix, 0.0)
        contrib = (picked * weight[:, None]).reshape(TOKENS, 2, D).sum(axis=1)
        return total + contrib, None

    total, _ = lax.scan(one_expert, jnp.zeros((TOKENS, D), jnp.float32), labels)
    return total.astype(jnp.bfloat16)
```

```python
import functools

import jax
import jax.numpy as jnp
from jax import lax
from jax.experimental import pallas as pl
from jax.experimental.pallas import tpu as pltpu
from jax.sharding import PartitionSpec as P

MESH = pl.DeviceIdType.MESH
BF16 = jnp.bfloat16
F32 = jnp.float32

COLS = 256
GROUPS = 1024 // COLS
PAIRS = COLS // 128
OFFSET = (0, 1, 2, 3, 4, 5, 6, 7, 8)
PARTS = ((0, 160), (160, 32))


def wrap(i, n):
    return lax.rem(i + n, n)


def kernel(
    tok_ref, ids_ref, logit_ref, gate_hbm, up_hbm, down_hbm, out_ref,
    gate_raw, up_raw, down_raw, gate_t, up_t, down_t,
    x_buf, p_buf, hidden, sel, w_high, w_low,
    disp_send, disp_recv, ret_send, ret_recv,
    a1, a2, a3, a4, b1, b2, b3, b4,
    weight_sem, disp_ss, disp_rs, ret_ss, ret_rs, ss, rs,
):
    me = lax.axis_index("expert")
    place = lax.axis_index("split")
    x = me // 4
    z_lo = lax.rem(me // 2, 2)
    z = place // 4
    y = lax.rem(place, 4)
    land = ((a1, a2, a3, a4), (b1, b2, b3, b4))

    def at_z(zz):
        return (me, wrap(zz, 4) * 4 + y)

    def at_y(yy):
        return (me, z * 4 + wrap(yy, 4))

    barrier = pltpu.get_barrier_semaphore()
    for d in range(1, 16):
        pl.semaphore_signal(barrier, inc=1, device_id=(wrap(me + d, 16), place), device_id_type=MESH)
    for dev in (at_z(z + 1), at_z(z - 1), at_y(y + 1), at_y(y - 1)):
        pl.semaphore_signal(barrier, inc=1, device_id=dev, device_id_type=MESH)

    loads = [
        pltpu.make_async_copy(src, dst, weight_sem.at[i])
        for i, (src, dst) in enumerate(((gate_hbm, gate_raw), (up_hbm, up_raw), (down_hbm, down_raw)))
    ]
    for c in loads:
        c.start()

    ids = ids_ref[...]
    labels = lax.broadcasted_iota(jnp.int32, (16, 256), 0)
    hit0 = ids[0:1, :] == labels
    hit1 = ids[1:2, :] == labels
    hits = jnp.where(hit0 | hit1, 1.0, 0.0).astype(F32)
    earlier = lax.broadcasted_iota(jnp.int32, (256, 256), 0) < lax.broadcasted_iota(jnp.int32, (256, 256), 1)
    count = jnp.dot(hits.astype(BF16), jnp.where(earlier, 1.0, 0.0).astype(BF16), preferred_element_type=F32)
    slot = jnp.where(hits > 0.5, count, -1.0).astype(jnp.int32)
    logits = logit_ref[...]
    first = 1.0 / (1.0 + jnp.exp(logits[1:2, :] - logits[0:1, :]))
    weight = jnp.where(hit0, first, jnp.where(hit1, 1.0 - first, 0.0))
    sub = lax.broadcasted_iota(jnp.int32, (64, 256), 0)
    zero = jnp.zeros((64, 256), BF16)
    for e in range(16):
        low, mid, high = e * 128, e * 128 + 64, e * 128 + 128
        one = jnp.where(sub == slot[e:e + 1, :], 1.0, 0.0).astype(BF16)
        sel[low:mid, 0:256] = one
        sel[low:mid, 256:512] = zero
        sel[mid:high, 0:256] = zero
        sel[mid:high, 256:512] = one

    tok = tok_ref[...]
    halves = jnp.concatenate([tok[0:96, :], tok[96:192, :]], axis=1)
    for e in range(16):
        disp_send[e] = lax.dot_general(
            halves, sel[e * 128:e * 128 + 128, :], (((1,), (1,)), ((), ())), preferred_element_type=F32
        ).astype(BF16)
    disp_recv[pl.ds(me, 1)] = disp_send[pl.ds(me, 1)]

    def dispatch(d):
        step, inner = d // 4, d % 4
        far = (0, 1, 3, 2)[step]
        target = wrap(x + far, 4) * 4 + wrap(me - x * 4 + inner, 4)
        return pltpu.make_async_remote_copy(
            src_ref=disp_send.at[target], dst_ref=disp_recv.at[me], send_sem=disp_ss.at[d],
            recv_sem=disp_rs.at[me], device_id=(target, place), device_id_type=MESH)

    pl.semaphore_wait(barrier, 19)
    for d in range(1, 16):
        dispatch(d).start()

    for e in range(16):
        low, mid, high = e * 128, e * 128 + 64, e * 128 + 128
        w = weight[e:e + 1, :]
        full = jnp.where(sub == slot[e:e + 1, :], w, 0.0)
        top = full.astype(BF16)
        rest = (full - top.astype(F32)).astype(BF16)
        for ref, val in ((w_high, top), (w_low, rest)):
            ref[low:mid, 0:256] = val
            ref[low:mid, 256:512] = zero
            ref[mid:high, 0:256] = zero
            ref[mid:high, 256:512] = val

    def pick(ref, g, part, i, j, r0, rows):
        zi, yi = (i, j) if part == 0 else (j, i)
        return ref.at[g, zi, yi, pl.ds(r0, rows), :]

    def coords(part):
        return (z, y) if part == 0 else (y, z)

    def device(part, axis, i):
        return at_z(i) if (axis == 0) == (part == 0) else at_y(i)

    def gather_refs(part, step, sign, g, arriving):
        u, v = coords(part)
        r0, rows = PARTS[part]
        half = rows // 2
        du, dv = (-sign, -sign) if arriving else (0, 0)
        lo = sign > 0
        if step == 0:
            return pick(x_buf, g, part, wrap(u + du, 4), v, r0, rows)
        if step == 1:
            return pick(x_buf, g, part, wrap(u - sign + du + 4, 4), v, r0 if lo else r0 + half, half)
        if step == 2:
            return pick(x_buf, g, part, slice(0, 4), wrap(v + dv, 4), r0, rows)
        return pick(x_buf, g, part, slice(0, 2) if lo else slice(2, 4), wrap(v - sign + dv + 4, 4), r0, rows)

    def gather(part, step, sign, g):
        u, v = coords(part)
        ref = gather_refs(part, step, sign, g, False)
        axis = 0 if step < 2 else 1
        k = step * 2 + (0 if sign > 0 else 1)
        return pltpu.make_async_remote_copy(
            src_ref=ref, dst_ref=ref, send_sem=ss.at[g, part, k], recv_sem=rs.at[g, part, k],
            device_id=device(part, axis, (u if axis == 0 else v) + sign), device_id_type=MESH)

    def gather_wait(part, step, sign, g):
        u, v = coords(part)
        ref = gather_refs(part, step, sign, g, True)
        axis = 0 if step < 2 else 1
        k = step * 2 + (0 if sign > 0 else 1)
        pltpu.make_async_remote_copy(
            src_ref=ref, dst_ref=ref, send_sem=ss.at[g, part, k], recv_sem=rs.at[g, part, k],
            device_id=device(part, axis, (u if axis == 0 else v) + sign), device_id_type=MESH).wait_recv()

    def scatter(part, step, sign, g):
        u, v = coords(part)
        r0, rows = PARTS[part]
        half = rows // 2
        lo = sign > 0
        side = 0 if lo else 1
        if step == 0:
            src = pick(p_buf, g, part, slice(0, 2) if lo else slice(2, 4), wrap(v + 2, 4), r0, rows)
        elif step == 1:
            src = pick(p_buf, g, part, slice(0, 4), wrap(v + sign, 4), r0, rows)
        elif step == 2:
            src = pick(p_buf, g, part, wrap(u + 2, 4), v, r0 if lo else r0 + half, half)
        else:
            src = pick(p_buf, g, part, wrap(u + sign, 4), v, r0, rows)
        axis = 1 if step < 2 else 0
        k = 8 + step * 2 + side
        return pltpu.make_async_remote_copy(
            src_ref=src, dst_ref=land[part][step].at[g, side], send_sem=ss.at[g, part, k], recv_sem=rs.at[g, part, k],
            device_id=device(part, axis, (u if axis == 0 else v) + sign), device_id_type=MESH)

    def add_into(ref, *others):
        total = ref[...].astype(F32)
        for o in others:
            total = total + o[...].astype(F32)
        ref[...] = total.astype(BF16)

    BOTH = ((0, 1), (0, -1), (1, 1), (1, -1))

    def blocks_of(g, i):
        q = g * PAIRS + i
        h = q // 2
        far = h + (h // 2) * (1 - 2 * lax.rem(h, 2))
        return lax.rem(x + far, 4) * 4 + lax.rem(z_lo + lax.rem(q, 2), 2) * 2

    def arrive(g):
        for i in range(PAIRS):
            b0 = blocks_of(g, i)
            for b in (b0, b0 + 1):
                @pl.when(b != me)
                def _():
                    pltpu.make_async_remote_copy(
                        src_ref=disp_send.at[b], dst_ref=disp_recv.at[b], send_sem=disp_ss.at[0],
                        recv_sem=disp_rs.at[b], device_id=(b, place), device_id_type=MESH).wait_recv()
            one, two = disp_recv[b0], disp_recv[b0 + 1]
            x_buf[g, z, y, 0:96, i * 128:i * 128 + 128] = jnp.concatenate([one[:, :64], two[:, :64]], axis=1)
            x_buf[g, z, y, 96:192, i * 128:i * 128 + 128] = jnp.concatenate([one[:, 64:], two[:, 64:]], axis=1)

    def multiply(g):
        rows = x_buf[g].reshape(3072, COLS)

        @pl.loop(0, 2)
        def _(i):
            m = pl.ds(pl.multiple_of(i * 256, 256), 256)
            gate = jnp.dot(gate_t[m, :], rows, preferred_element_type=F32)
            up = jnp.dot(up_t[m, :], rows, preferred_element_type=F32)
            hidden[m, :] = (gate / (1.0 + jnp.exp(-gate)) * up).astype(BF16)

        @pl.loop(0, 4)
        def _(i):
            m = pl.ds(pl.multiple_of(i * 768, 768), 768)
            part = jnp.dot(down_t[m, :], hidden[...], preferred_element_type=F32)
            p_buf[g, i] = part.astype(BF16).reshape(4, 192, COLS)

    def give_back(g):
        rows = []
        for part in (0, 1):
            u, v = coords(part)
            r0, n = PARTS[part]
            total = pick(p_buf, g, part, u, v, r0, n)[...].astype(F32)
            total = total + land[part][3][g, 0].astype(F32) + land[part][3][g, 1].astype(F32)
            rows.append(total.astype(BF16))
        whole = jnp.concatenate(rows, axis=0)
        for i in range(PAIRS):
            b0 = blocks_of(g, i)
            tile = whole[:, i * 128:i * 128 + 128]
            for k in (0, 1):
                lanes = slice(k * 64, k * 64 + 64)
                ret_send[g, i, k] = jnp.concatenate([tile[0:96, lanes], tile[96:192, lanes]], axis=1)

                @pl.when(b0 + k != me)
                def _():
                    returning(g, i, k).start()

                @pl.when(b0 + k == me)
                def _():
                    ret_recv[pl.ds(me, 1)] = ret_send[g, i, pl.ds(k, 1)]

    def returning(g, i, k):
        target = blocks_of(g, i) + k
        return pltpu.make_async_remote_copy(
            src_ref=ret_send.at[g, i, k], dst_ref=ret_recv.at[me], send_sem=ret_ss.at[g, i, k],
            recv_sem=ret_rs.at[me], device_id=(target, place), device_id_type=MESH)

    def stage(k, g):
        if k == 0:
            arrive(g)
            for part, sign in BOTH:
                gather(part, 0, sign, g).start()
        elif k < 4:
            for part, sign in BOTH:
                gather_wait(part, k - 1, sign, g)
            for part, sign in BOTH:
                gather(part, k, sign, g).start()
        elif k == 4:
            for part, sign in BOTH:
                gather_wait(part, 3, sign, g)
            multiply(g)
            for part, sign in BOTH:
                scatter(part, 0, sign, g).start()
        else:
            step = k - 5
            for part, sign in BOTH:
                scatter(part, step, sign, g).wait_recv()
            if k == 8:
                give_back(g)
                return
            for part in (0, 1):
                u, v = coords(part)
                r0, n = PARTS[part]
                half = n // 2
                got = land[part][step]
                if step == 0:
                    add_into(pick(p_buf, g, part, slice(0, 2), wrap(v + 1, 4), r0, n), got.at[g, 0])
                    add_into(pick(p_buf, g, part, slice(2, 4), wrap(v - 1, 4), r0, n), got.at[g, 1])
                elif step == 1:
                    add_into(pick(p_buf, g, part, slice(0, 4), v, r0, n), got.at[g, 0], got.at[g, 1])
                else:
                    add_into(pick(p_buf, g, part, wrap(u + 1, 4), v, r0, half), got.at[g, 0])
                    add_into(pick(p_buf, g, part, wrap(u - 1, 4), v, r0 + half, half), got.at[g, 1])
                for sign in (1, -1):
                    scatter(part, step + 1, sign, g).start()

    def tick(t):
        for k in range(8, -1, -1):
            g = t - OFFSET[k]

            @pl.when((g >= 0) & (g < GROUPS))
            def _():
                stage(k, g)

    def prepare():
        for c in loads:
            c.wait()

        @pl.loop(0, 12)
        def _(i):
            m = pl.ds(pl.multiple_of(i * 256, 256), 256)
            gate_t[:, m] = gate_raw[m, :].T
            up_t[:, m] = up_raw[m, :].T
            down_t[m, :] = down_raw[:, m].T

    pl.loop(0, 2)(tick)
    prepare()
    pl.loop(2, OFFSET[8] + GROUPS)(tick)

    for d in range(1, 16):
        src = wrap(me + d, 16)
        pltpu.make_async_remote_copy(
            src_ref=disp_send.at[src], dst_ref=ret_recv.at[src], send_sem=disp_ss.at[0],
            recv_sem=ret_rs.at[src], device_id=(src, place), device_id_type=MESH).wait_recv()
    back = jnp.concatenate([ret_recv[e] for e in range(16)], axis=1)
    mixed = jnp.dot(back, w_high[...], preferred_element_type=F32) + jnp.dot(
        back, w_low[...], preferred_element_type=F32)
    out_ref[0:96, :] = mixed[:, 0:256].astype(BF16)
    out_ref[96:192, :] = mixed[:, 256:512].astype(BF16)

    for d in range(1, 16):
        dispatch(d).wait_send()

    @pl.loop(0, GROUPS)
    def _(g):
        for part, sign in BOTH:
            for step in range(4):
                gather(part, step, sign, g).wait_send()
                scatter(part, step, sign, g).wait_send()
        for i in range(PAIRS):
            for k in (0, 1):
                @pl.when(blocks_of(g, i) + k != me)
                def _():
                    returning(g, i, k).wait_send()


def body(tokens, expert_ids, pair_logits, gate_weight, up_weight, down_weight):
    vmem = pl.BlockSpec(memory_space=pltpu.VMEM)
    hbm = pl.BlockSpec(memory_space=pl.ANY)
    dma = pltpu.SemaphoreType.DMA
    landing = []
    for part in (0, 1):
        n = PARTS[part][1]
        landing += [
            pltpu.VMEM((GROUPS, 2, 2, n, COLS), BF16),
            pltpu.VMEM((GROUPS, 2, 4, n, COLS), BF16),
            pltpu.VMEM((GROUPS, 2, n // 2, COLS), BF16),
            pltpu.VMEM((GROUPS, 2, n, COLS), BF16),
        ]
    out = pl.pallas_call(
        kernel,
        out_shape=jax.ShapeDtypeStruct((192, 256), BF16),
        in_specs=[vmem, vmem, vmem, hbm, hbm, hbm],
        out_specs=vmem,
        scratch_shapes=[
            pltpu.VMEM((3072, 512), BF16), pltpu.VMEM((3072, 512), BF16), pltpu.VMEM((512, 3072), BF16),
            pltpu.VMEM((512, 3072), BF16), pltpu.VMEM((512, 3072), BF16), pltpu.VMEM((3072, 512), BF16),
            pltpu.VMEM((GROUPS, 4, 4, 192, COLS), BF16), pltpu.VMEM((GROUPS, 4, 4, 192, COLS), BF16),
            pltpu.VMEM((512, COLS), BF16),
            pltpu.VMEM((2048, 512), BF16), pltpu.VMEM((2048, 512), BF16), pltpu.VMEM((2048, 512), BF16),
            pltpu.VMEM((16, 96, 128), BF16), pltpu.VMEM((16, 96, 128), BF16),
            pltpu.VMEM((GROUPS, PAIRS, 2, 96, 128), BF16), pltpu.VMEM((16, 96, 128), BF16),
            *landing,
            dma((3,)), dma((16,)), dma((16,)), dma((GROUPS, PAIRS, 2)), dma((16,)),
            dma((GROUPS, 2, 16)), dma((GROUPS, 2, 16)),
        ],
        compiler_params=pltpu.CompilerParams(
            collective_id=0, has_side_effects=True, vmem_limit_bytes=60 * 2**20),
        cost_estimate=pl.CostEstimate(flops=9_700_000_000, bytes_accessed=10_000_000, transcendentals=524288),
    )(tokens.T, expert_ids.T, pair_logits.T, gate_weight[0], up_weight[0], down_weight[0])
    return out.T


def solution(mesh):
    in_specs = (
        P("expert", "split"),
        P("expert", None),
        P("expert", None),
        P("expert", None, "split"),
        P("expert", None, "split"),
        P("expert", "split", None),
    )
    return jax.shard_map(body, mesh=mesh, in_specs=in_specs, out_specs=P("expert", "split"), check_vma=False)
```

```python
import functools

import jax
import jax.numpy as jnp
from jax import lax
from jax.experimental import pallas as pl
from jax.experimental.pallas import tpu as pltpu
from jax.sharding import PartitionSpec as P

MESH = pl.DeviceIdType.MESH
BF16 = jnp.bfloat16
F32 = jnp.float32

COLS = 256
GROUPS = 4
PARTS = ((0, 128),)
RA = 128
RC = 64
HA, HC = RA // 2, RC // 2
ORDER = (
    ("g", 0, 0, 0), ("h", 1), ("h", 2), ("g", 1, 0, 0), ("g", 0, 1, 0), ("g", 2, 0, 0),
    ("h", 3), ("prep", 3), ("prep", 0), ("prep", 1), ("tab",), ("g", 1, 1, 0),
    ("h", 4), ("g", 2, 1, 0), ("g", 0, 3, 0), ("h", 5), ("g", 3, 0, 0), ("g", 1, 3, 0),
    ("pk", 1), ("g", 3, 1, 0), ("pk", 3), ("g", 2, 3, 0), ("prep", 2), ("g", 0, 2, 0),
    ("pk", 0), ("mu", 0), ("mc", 0), ("ma", 0), ("g", 1, 2, 0), ("pk", 2),
    ("g", 2, 2, 0), ("add", 0), ("g", 3, 3, 0), ("mu", 1), ("mc", 1), ("ma", 1),
    ("mu", 3), ("g", 3, 2, 0), ("mc", 3), ("s", 1, 0, 0), ("ma", 3), ("mu", 2),
    ("s", 1, 1, 0), ("mc", 2), ("s", 2, 0, 0), ("s", 3, 0, 0), ("s", 1, 3, 0), ("ma", 2),
    ("s", 2, 1, 0), ("s", 4, 0, 0), ("s", 3, 1, 0), ("add", 1), ("add", 3), ("add", 2),
    ("t", 0), ("s", 2, 3, 0), ("t", 1), ("s", 1, 2, 0), ("s", 3, 3, 0), ("s", 4, 1, 0),
    ("t", 2), ("s", 4, 3, 0), ("s", 2, 2, 0), ("t", 3), ("s", 3, 2, 0), ("own",),
    ("t", 4), ("s", 4, 2, 0), ("t", 5),
)
FAR = (0, 1, 3, 2)


def wrap(i, n):
    return lax.rem(i + n, n)


def kernel(
    tok_ref, ids_ref, logit_ref, gate_hbm, up_hbm, down_hbm, out_ref,
    gate_raw, up_raw, down_raw, gate_t, up_t, down_t,
    xa, pa, hidden, sel, w_high, w_low,
    disp_send, disp_recv, ret_send, ret_recv, a1, a2, a3, a4,
    meta, slots, mixes, sel_c, wc_high, wc_low,
    raw, xs, xc, pc, tr, acc, tsum, z1, z2, z3, z4, y1, y2,
    weight_sem, disp_ss, disp_rs, ret_ss, ret_rs, ss, rs, cs, cr, xss, xrs, tss, trs, local_sem,
):
    me = lax.axis_index("expert")
    place = lax.axis_index("split")
    x = me // 4
    zl = lax.rem(me // 2, 2)
    c = lax.rem(me, 2)
    z = place // 4
    y = lax.rem(place, 4)
    z8 = z * 2 + zl

    def at_z(zz):
        return (me, wrap(zz, 4) * 4 + y)

    def at_y(yy):
        return (me, z * 4 + wrap(yy, 4))

    def at_z8(zz):
        w = wrap(zz, 8)
        return (x * 4 + lax.rem(w, 2) * 2 + c, (w // 2) * 4 + y)

    def at_x(r, core):
        return (lax.rem(x + r, 4) * 4 + zl * 2 + core, place)

    def remote(src, dst, send, recv, dev):
        return pltpu.make_async_remote_copy(
            src_ref=src, dst_ref=dst, send_sem=send, recv_sem=recv, device_id=dev, device_id_type=MESH)

    barrier = pltpu.get_barrier_semaphore()
    for d in range(1, 16):
        pl.semaphore_signal(barrier, inc=1, device_id=(wrap(me + d, 16), place), device_id_type=MESH)
    for dev in (at_z(z + 1), at_z(z - 1), at_y(y + 1), at_y(y - 1), at_z8(z8 + 2 * zl - 1)):
        pl.semaphore_signal(barrier, inc=1, device_id=dev, device_id_type=MESH)

    loads = [
        pltpu.make_async_copy(src, dst, weight_sem.at[i])
        for i, (src, dst) in enumerate(((gate_hbm, gate_raw), (up_hbm, up_raw), (down_hbm, down_raw)))
    ]
    for load in loads:
        load.start()

    tok = tok_ref[...]
    raw[z8, y] = tok[RA:, :]
    meta[zl, 0:2, :] = ids_ref[...].astype(F32)
    meta[zl, 2:4, :] = logit_ref[...]
    meta[zl, 4:8, :] = jnp.zeros((4, 256), F32)

    def swap_meta():
        return remote(meta.at[zl], meta.at[zl], cs.at[24], cr.at[24], (x * 4 + (1 - zl) * 2 + c, place))

    def head(step, sign, arriving=False):
        lo = sign > 0
        k = step * 2 + (0 if lo else 1)
        back = -sign if arriving else 0
        if step == 0:
            ref = raw.at[z8, wrap(y + back, 4)]
        elif step == 1:
            ref = raw.at[z8, wrap(y - sign + back + 4, 4), pl.ds(0 if lo else HC, HC)]
        else:
            n = step - 2
            chunk = wrap(z8 - sign * n + back + 8, 8)
            ref = raw.at[chunk] if n < 3 else raw.at[chunk, pl.ds(0 if lo else 2, 2)]
        return remote(ref, ref, cs.at[k], cr.at[k], at_y(y + sign) if step < 2 else at_z8(z8 + sign))

    def head_step(step):
        for sign in (1, -1):
            head(step - 1, sign, True).wait_recv()
        for sign in (1, -1):
            head(step, sign).start()

    labels = lax.broadcasted_iota(jnp.int32, (16, 256), 0).astype(F32)
    earlier = lax.broadcasted_iota(jnp.int32, (256, 256), 0) < lax.broadcasted_iota(jnp.int32, (256, 256), 1)
    earlier = jnp.where(earlier, 1.0, 0.0).astype(BF16)
    sub = lax.broadcasted_iota(jnp.int32, (64, 256), 0).astype(F32)
    zero = jnp.zeros((64, 256), BF16)

    def slot_of(ids):
        hits = jnp.where((ids[0:1, :] == labels) | (ids[1:2, :] == labels), 1.0, 0.0)
        count = jnp.dot(hits.astype(BF16), earlier, preferred_element_type=F32)
        return jnp.where(hits > 0.5, count, -1.0)

    def mix_of(ids, logits):
        first = 1.0 / (1.0 + jnp.exp(logits[1:2, :] - logits[0:1, :]))
        return jnp.where(ids[0:1, :] == labels, first, jnp.where(ids[1:2, :] == labels, 1.0 - first, 0.0))

    ids = ids_ref[...].astype(F32)
    slot = slot_of(ids)
    mix = mix_of(ids, logit_ref[...])

    def one_hot(row):
        return jnp.where(sub == row, 1.0, 0.0).astype(BF16)

    def split(row, w):
        full = jnp.where(sub == row, w, 0.0)
        top = full.astype(BF16)
        return top, (full - top.astype(F32)).astype(BF16)

    def place_two(ref, base, first, second):
        ref[base:base + 64, 0:256] = first
        ref[base:base + 64, 256:512] = zero
        ref[base + 64:base + 128, 0:256] = zero
        ref[base + 64:base + 128, 256:512] = second

    for e in range(16):
        one = one_hot(slot[e:e + 1, :])
        place_two(sel, e * 128, one, one)

    halves = jnp.concatenate([tok[0:HA, :], tok[HA:RA, :]], axis=1)
    for e in range(16):
        disp_send[e] = lax.dot_general(
            halves, sel[e * 128:e * 128 + 128, :], (((1,), (1,)), ((), ())), preferred_element_type=F32
        ).astype(BF16)
    disp_recv[pl.ds(me, 1)] = disp_send[pl.ds(me, 1)]

    def dispatch(d):
        step, inner = d // 4, d % 4
        target = wrap(x + FAR[step], 4) * 4 + wrap(me - x * 4 + inner, 4)
        return remote(disp_send.at[target], disp_recv.at[me], disp_ss.at[d], disp_rs.at[me], (target, place))

    pl.semaphore_wait(barrier, 20)
    swap_meta().start()
    for sign in (1, -1):
        head(0, sign).start()
    for d in range(1, 16):
        dispatch(d).start()

    def tables():
        remote(meta.at[zl], meta.at[1 - zl], cs.at[24], cr.at[24], (x * 4 + (1 - zl) * 2 + c, place)).wait_recv()
        for b in (0, 1):
            both = meta[b]
            slots[b] = slot_of(both[0:2])
            mixes[b] = mix_of(both[0:2], both[2:4])
        for r in range(4):
            for core in (0, 1):
                e = lax.rem(x + r, 4) * 4 + zl * 2 + core
                base = r * 256 + core * 128
                row = [slots[b, pl.ds(e, 1), :] for b in (0, 1)]
                w = [mixes[b, pl.ds(e, 1), :] for b in (0, 1)]
                place_two(sel_c, base, one_hot(row[0]), one_hot(row[1]))
                first, second = split(row[0], w[0]), split(row[1], w[1])
                place_two(wc_high, base, first[0], second[0])
                place_two(wc_low, base, first[1], second[1])

    def own_weights():
        for e in range(16):
            top, rest = split(slot[e:e + 1, :], mix[e:e + 1, :])
            place_two(w_high, e * 128, top, top)
            place_two(w_low, e * 128, rest, rest)

    def x_out(r, core):
        return remote(xs.at[r, core], xc.at[(4 - r) % 4, c], xss.at[r, core], xrs.at[(4 - r) % 4, c], at_x(r, core))

    def x_back(r, core):
        return remote(pc.at[r, core], tr.at[(4 - r) % 4, c], tss.at[r, core], trs.at[(4 - r) % 4, c], at_x(r, core))

    def keep(out):
        src, dst, i = (xs.at[0, c], xc.at[0, c], 0) if out else (pc.at[0, c], tr.at[0, c], 1)
        return pltpu.make_async_copy(src, dst, local_sem.at[i])

    def x_arrived(refs, sems, r, core):
        remote(refs.at[r, core], refs.at[r, core], xss.at[0, 0], sems.at[r, core], at_x(r, core)).wait_recv()

    def pick_slots(r):
        base = r * 256

        @pl.loop(0, 4)
        def _(i):
            first = raw[i * 2].reshape(4 * RC, 256)
            second = raw[i * 2 + 1].reshape(4 * RC, 256)
            got = lax.dot_general(
                first, sel_c[base:base + 256, 0:256], (((1,), (1,)), ((), ())), preferred_element_type=F32)
            got = got + lax.dot_general(
                second, sel_c[base:base + 256, 256:512], (((1,), (1,)), ((), ())), preferred_element_type=F32)
            got = got.astype(BF16)
            s = pl.ds(i * 4, 4)
            xs[r, 0, s] = got[:, :128].reshape(4, RC, 128)
            xs[r, 1, s] = got[:, 128:].reshape(4, RC, 128)

        if r == 0:
            keep(True).start()
            x_out(0, 1 - c).start()
        else:
            for core in (0, 1):
                x_out(r, core).start()

    def wait_slots(r):
        if r == 0:
            keep(True).wait()
            x_arrived(xc, xrs, 0, 1 - c)
        else:
            for core in (0, 1):
                x_arrived(xc, xrs, r, core)

    def add_up(r, first, last):
        if r == 0:
            keep(False).wait()
            x_arrived(tr, trs, 0, 1 - c)
        else:
            for core in (0, 1):
                x_arrived(tr, trs, r, core)

        @pl.loop(0, 4)
        def _(i):
            s = pl.ds(i * 4, 4)
            rows = jnp.concatenate(
                [tr[r, 0, s].reshape(4 * RC, 128), tr[r, 1, s].reshape(4 * RC, 128)], axis=1)
            base = r * 256
            total = jnp.dot(rows, wc_high[base:base + 256, :], preferred_element_type=F32)
            total = total + jnp.dot(rows, wc_low[base:base + 256, :], preferred_element_type=F32)
            if not first:
                total = total + acc[i]
            if last:
                total = total.astype(BF16)
                tsum[i * 2] = total[:, 0:256].reshape(4, RC, 256)
                tsum[i * 2 + 1] = total[:, 256:512].reshape(4, RC, 256)
            else:
                acc[i] = total

    def add_into(ref, *others):
        total = ref[...].astype(F32)
        for o in others:
            total = total + o[...].astype(F32)
        ref[...] = total.astype(BF16)

    tail_land = (z1, z2, z3, z4, y1, y2)

    def tail(step, sign):
        lo = sign > 0
        side = 0 if lo else 1
        k = 12 + step * 2 + side
        if step == 0:
            src = tsum.at[wrap(z8 + 4, 8), pl.ds(0 if lo else 2, 2)]
        elif step < 4:
            src = tsum.at[wrap(z8 + sign * (4 - step), 8)]
        elif step == 4:
            src = tsum.at[z8, wrap(y + 2, 4), pl.ds(0 if lo else HC, HC)]
        else:
            src = tsum.at[z8, wrap(y + sign, 4)]
        return remote(src, tail_land[step].at[side], cs.at[k], cr.at[k],
                      at_z8(z8 + sign) if step < 4 else at_y(y + sign))

    def tail_step(step):
        if step > 0:
            for sign in (1, -1):
                tail(step - 1, sign).wait_recv()
        got = tail_land[step - 1]
        if step == 1:
            add_into(tsum.at[wrap(z8 + 3, 8), pl.ds(0, 2)], got.at[0])
            add_into(tsum.at[wrap(z8 - 3, 8), pl.ds(2, 2)], got.at[1])
        elif step in (2, 3):
            add_into(tsum.at[wrap(z8 + 4 - step, 8)], got.at[0])
            add_into(tsum.at[wrap(z8 - 4 + step, 8)], got.at[1])
        elif step == 4:
            add_into(tsum.at[z8], got.at[0], got.at[1])
        elif step == 5:
            add_into(tsum.at[z8, wrap(y + 1, 4), pl.ds(0, HC)], got.at[0])
            add_into(tsum.at[z8, wrap(y - 1, 4), pl.ds(HC, HC)], got.at[1])
        for sign in (1, -1):
            tail(step, sign).start()

    land = ((a1, a2, a3, a4),)

    def at_part(ref, r, part, i, j, half=None):
        r0, n = PARTS[part]
        zi, yi = (i, j) if part == 0 else (j, i)
        if half is None:
            return ref.at[r, zi, yi, pl.ds(r0, n)]
        if n % 32 == 0:
            return ref.at[r, zi, yi, pl.ds(r0 + half * (n // 2), n // 2)]
        return ref.at[r, zi, yi, pl.ds(r0, n), pl.ds(half * 128, 128)]

    def coords(part):
        return (z, y) if part == 0 else (y, z)

    def device(part, axis, i):
        return at_z(i) if axis == part else at_y(i)

    ALL, LOW, HIGH = pl.ds(0, 4), pl.ds(0, 2), pl.ds(2, 2)

    def gather(part, step, sign, r, arriving=False):
        u, v = coords(part)
        back = -sign if arriving else 0
        lo = sign > 0
        if step == 0:
            ref = at_part(xa, r, part, wrap(u + back, 4), v)
        elif step == 1:
            ref = at_part(xa, r, part, wrap(u - sign + back + 4, 4), v, 0 if lo else 1)
        elif step == 2:
            ref = at_part(xa, r, part, ALL, wrap(v + back, 4))
        else:
            ref = at_part(xa, r, part, LOW if lo else HIGH, wrap(v - sign + back + 4, 4))
        k = step * 2 + (0 if lo else 1)
        axis = 0 if step < 2 else 1
        return remote(ref, ref, ss.at[r, part, k], rs.at[r, part, k],
                      device(part, axis, (u if axis == 0 else v) + sign))

    def scatter(part, step, sign, r):
        u, v = coords(part)
        lo = sign > 0
        side = 0 if lo else 1
        if step == 0:
            src = at_part(pa, r, part, LOW if lo else HIGH, wrap(v + 2, 4))
        elif step == 1:
            src = at_part(pa, r, part, ALL, wrap(v + sign, 4))
        elif step == 2:
            src = at_part(pa, r, part, wrap(u + 2, 4), v, side)
        else:
            src = at_part(pa, r, part, wrap(u + sign, 4), v)
        k = 8 + step * 2 + side
        axis = 1 if step < 2 else 0
        return remote(src, land[part][step].at[r, side], ss.at[r, part, k], rs.at[r, part, k],
                      device(part, axis, (u if axis == 0 else v) + sign))

    def block_of(r, core, b):
        return lax.rem(x + r, 4) * 4 + b * 2 + core

    def arrive(r):
        for core in (0, 1):
            for b in (0, 1):
                src = block_of(r, core, b)

                @pl.when(src != me)
                def _():
                    remote(disp_recv.at[src], disp_recv.at[src], disp_ss.at[0], disp_rs.at[src],
                           (src, place)).wait_recv()
            one, two = disp_recv[block_of(r, core, 0)], disp_recv[block_of(r, core, 1)]
            lanes = slice(core * 128, core * 128 + 128)
            xa[r, z, y, 0:HA, lanes] = jnp.concatenate([one[:, :64], two[:, :64]], axis=1)
            xa[r, z, y, HA:RA, lanes] = jnp.concatenate([one[:, 64:], two[:, 64:]], axis=1)

    def units(r):
        for part in range(len(PARTS)):
            for sign in (1, -1):
                gather(part, 3, sign, r, True).wait_recv()
        wait_slots(r)
        rows = xa[r].reshape(16 * RA, COLS)
        more = jnp.concatenate([xc[r, 0].reshape(16 * RC, 128), xc[r, 1].reshape(16 * RC, 128)], axis=1)

        @pl.loop(0, 2)
        def _(i):
            m = pl.ds(pl.multiple_of(i * 256, 256), 256)

            def product(w):
                return jnp.dot(w[m, 0:16 * RA], rows, preferred_element_type=F32) + jnp.dot(
                    w[m, 16 * RA:], more, preferred_element_type=F32)

            gate, up = product(gate_t), product(up_t)
            hidden[m, :] = (gate / (1.0 + jnp.exp(-gate)) * up).astype(BF16)

    def results_c(r):
        @pl.loop(0, 2)
        def _(i):
            m = pl.ds(pl.multiple_of(16 * RA + i * 8 * RC, 128), 8 * RC)
            part = jnp.dot(down_t[m, :], hidden[...], preferred_element_type=F32).astype(BF16)
            s = pl.ds(i * 8, 8)
            pc[r, 0, s] = part[:, :128].reshape(8, RC, 128)
            pc[r, 1, s] = part[:, 128:].reshape(8, RC, 128)

        if r == 0:
            keep(False).start()
            x_back(0, 1 - c).start()
        else:
            for core in (0, 1):
                x_back(r, core).start()

    def results_a(r):
        @pl.loop(0, 4)
        def _(i):
            m = pl.ds(pl.multiple_of(i * 4 * RA, 128), 4 * RA)
            part = jnp.dot(down_t[m, :], hidden[...], preferred_element_type=F32)
            pa[r, i] = part.astype(BF16).reshape(4, RA, COLS)

        for part in range(len(PARTS)):
            for sign in (1, -1):
                scatter(part, 0, sign, r).start()

    def returning(r, core, b):
        target = block_of(r, core, b)
        return remote(ret_send.at[r, core, b], ret_recv.at[me], ret_ss.at[r, core, b], ret_rs.at[me], (target, place))

    def give_back(r):
        rows = []
        for part, (r0, n) in enumerate(PARTS):
            last = land[part][3]
            total = pa[r, z, y, r0:r0 + n].astype(F32) + last[r, 0].astype(F32) + last[r, 1].astype(F32)
            rows.append(total.astype(BF16))
        whole = jnp.concatenate(rows, axis=0)
        for core in (0, 1):
            tile = whole[:, core * 128:core * 128 + 128]
            for b in (0, 1):
                lanes = slice(b * 64, b * 64 + 64)
                ret_send[r, core, b] = jnp.concatenate([tile[0:HA, lanes], tile[HA:RA, lanes]], axis=1)

                @pl.when(block_of(r, core, b) != me)
                def _():
                    returning(r, core, b).start()

                @pl.when(block_of(r, core, b) == me)
                def _():
                    ret_recv[pl.ds(me, 1)] = ret_send[r, core, pl.ds(b, 1)]

    def gather_op(step, r, part):
        if step == 0:
            if ("here", r) not in seen:
                seen.add(("here", r))
                arrive(r)
        else:
            for sign in (1, -1):
                gather(part, step - 1, sign, r, True).wait_recv()
        for sign in (1, -1):
            gather(part, step, sign, r).start()

    def scatter_op(step, r, part):
        for sign in (1, -1):
            scatter(part, step - 1, sign, r).wait_recv()
        if step == 4:
            seen.add(("summed", r, part))
            if all(("summed", r, p) in seen for p in range(len(PARTS))):
                give_back(r)
            return
        u, v = coords(part)
        got = land[part][step - 1]
        if step == 1:
            add_into(at_part(pa, r, part, LOW, wrap(v + 1, 4)), got.at[r, 0])
            add_into(at_part(pa, r, part, HIGH, wrap(v - 1, 4)), got.at[r, 1])
        elif step == 2:
            add_into(at_part(pa, r, part, ALL, v), got.at[r, 0], got.at[r, 1])
        else:
            add_into(at_part(pa, r, part, wrap(u + 1, 4), v, 0), got.at[r, 0])
            add_into(at_part(pa, r, part, wrap(u - 1, 4), v, 1), got.at[r, 1])
        for sign in (1, -1):
            scatter(part, step, sign, r).start()

    def prepare(i):
        m = pl.ds(pl.multiple_of(i * 384, 128), 384)
        wide = pl.multiple_of(i * 2 * RA, 128)
        thin = pl.multiple_of(16 * RA + i * 2 * RC, 128)
        for src, dst in ((gate_raw, gate_t), (up_raw, up_t)):
            w = src[m, :]
            dst[:, pl.ds(wide, RA)] = w[0:RA].T
            dst[:, pl.ds(wide + RA, RA)] = w[192:192 + RA].T
            dst[:, pl.ds(thin, 2 * RC)] = jnp.concatenate([w[RA:192], w[192 + RA:384]], axis=0).T
        w = down_raw[:, m].T
        down_t[pl.ds(wide, RA), :] = w[0:RA]
        down_t[pl.ds(wide + RA, RA), :] = w[192:192 + RA]
        down_t[pl.ds(thin, RC), :] = w[RA:192]
        down_t[pl.ds(thin + RC, RC), :] = w[192 + RA:384]

    seen = set()

    def loaded():
        if "loaded" not in seen:
            seen.add("loaded")
            for load in loads:
                load.wait()

    for op, *at in ORDER:
        if op == "h":
            head_step(*at)
        elif op == "pk":
            if "tokens" not in seen:
                seen.add("tokens")
                for sign in (1, -1):
                    head(5, sign, True).wait_recv()
            pick_slots(*at)
        elif op == "g":
            gather_op(*at)
        elif op == "mu":
            units(*at)
        elif op == "mc":
            results_c(*at)
        elif op == "ma":
            results_a(*at)
        elif op == "s":
            scatter_op(*at)
        elif op == "add":
            added = sum(1 for k in seen if k[0] == "add")
            seen.add(("add", *at))
            add_up(*at, added == 0, added == 3)
        elif op == "t":
            tail_step(*at)
        elif op == "prep":
            loaded()
            pl.loop(at[0] * 2, at[0] * 2 + 2)(prepare)
        elif op == "tab":
            tables()
        elif op == "own":
            own_weights()

    for sign in (1, -1):
        tail(5, sign).wait_recv()
    out_ref[RA:, :] = (tsum[z8, y].astype(F32) + y2[0].astype(F32) + y2[1].astype(F32)).astype(BF16)

    for d in range(1, 16):
        src = wrap(me + d, 16)
        remote(ret_recv.at[src], ret_recv.at[src], disp_ss.at[0], ret_rs.at[src], (src, place)).wait_recv()
    back = jnp.concatenate([ret_recv[e] for e in range(16)], axis=1)
    mixed = jnp.dot(back, w_high[...], preferred_element_type=F32) + jnp.dot(
        back, w_low[...], preferred_element_type=F32)
    out_ref[0:HA, :] = mixed[:, 0:256].astype(BF16)
    out_ref[HA:RA, :] = mixed[:, 256:512].astype(BF16)

    swap_meta().wait_send()
    for sign in (1, -1):
        for step in range(6):
            head(step, sign).wait_send()
            tail(step, sign).wait_send()
    x_out(0, 1 - c).wait_send()
    x_back(0, 1 - c).wait_send()
    for r in (1, 2, 3):
        for core in (0, 1):
            x_out(r, core).wait_send()
            x_back(r, core).wait_send()
    for d in range(1, 16):
        dispatch(d).wait_send()

    for r in range(GROUPS):
        for part in range(len(PARTS)):
            for sign in (1, -1):
                for step in range(4):
                    gather(part, step, sign, r).wait_send()
                    scatter(part, step, sign, r).wait_send()
        for core in (0, 1):
            for b in (0, 1):
                @pl.when(block_of(r, core, b) != me)
                def _():
                    returning(r, core, b).wait_send()


def body(tokens, expert_ids, pair_logits, gate_weight, up_weight, down_weight):
    vmem = pl.BlockSpec(memory_space=pltpu.VMEM)
    hbm = pl.BlockSpec(memory_space=pl.ANY)
    dma = pltpu.SemaphoreType.DMA

    def buf(*shape):
        return pltpu.VMEM(shape, BF16)

    def buf32(*shape):
        return pltpu.VMEM(shape, F32)

    landing = []
    for _, n in PARTS:
        half = (n // 2, COLS) if n % 32 == 0 else (n, 128)
        landing += [
            buf(GROUPS, 2, 2, n, COLS), buf(GROUPS, 2, 4, n, COLS), buf(GROUPS, 2, *half), buf(GROUPS, 2, n, COLS)]
    out = pl.pallas_call(
        kernel,
        out_shape=jax.ShapeDtypeStruct((192, 256), BF16),
        in_specs=[vmem, vmem, vmem, hbm, hbm, hbm],
        out_specs=vmem,
        scratch_shapes=[
            buf(3072, 512), buf(3072, 512), buf(512, 3072),
            buf(512, 3072), buf(512, 3072), buf(3072, 512),
            buf(GROUPS, 4, 4, RA, COLS), buf(GROUPS, 4, 4, RA, COLS), buf(512, COLS),
            buf(2048, 512), buf(2048, 512), buf(2048, 512),
            buf(16, HA, 128), buf(16, HA, 128), buf(GROUPS, 2, 2, HA, 128), buf(16, HA, 128),
            *landing,
            buf32(2, 8, 256), buf32(2, 16, 256), buf32(2, 16, 256),
            buf(1024, 512), buf(1024, 512), buf(1024, 512),
            buf(8, 4, RC, 256), buf(4, 2, 16, RC, 128), buf(4, 2, 16, RC, 128),
            buf(4, 2, 16, RC, 128), buf(4, 2, 16, RC, 128),
            buf32(4, 4 * RC, 512), buf(8, 4, RC, 256),
            buf(2, 2, RC, 256), buf(2, 4, RC, 256), buf(2, 4, RC, 256), buf(2, 4, RC, 256),
            buf(2, HC, 256), buf(2, RC, 256),
            dma((3,)), dma((16,)), dma((16,)), dma((GROUPS, 2, 2)), dma((16,)),
            dma((GROUPS, len(PARTS), 16)), dma((GROUPS, len(PARTS), 16)), dma((25,)), dma((25,)),
            dma((4, 2)), dma((4, 2)), dma((4, 2)), dma((4, 2)), dma((2,)),
        ],
        compiler_params=pltpu.CompilerParams(
            collective_id=0, has_side_effects=True, vmem_limit_bytes=60 * 2**20),
        cost_estimate=pl.CostEstimate(flops=9_700_000_000, bytes_accessed=10_000_000, transcendentals=524288),
    )(tokens.T, expert_ids.T, pair_logits.T, gate_weight[0], up_weight[0], down_weight[0])
    return out.T


def solution(mesh):
    in_specs = (
        P("expert", "split"),
        P("expert", None),
        P("expert", None),
        P("expert", None, "split"),
        P("expert", None, "split"),
        P("expert", "split", None),
    )
    return jax.shard_map(body, mesh=mesh, in_specs=in_specs, out_specs=P("expert", "split"), check_vma=False)
```

```python
import functools

import jax
import jax.numpy as jnp
from jax import lax
from jax.experimental import pallas as pl
from jax.experimental.pallas import tpu as pltpu
from jax.sharding import PartitionSpec as P

MESH = pl.DeviceIdType.MESH
BF16 = jnp.bfloat16
F32 = jnp.float32

COLS = 256
GROUPS = 4
PARTS = ((0, 128),)
RA = 128
RC = 64
HA, HC = RA // 2, RC // 2
ORDER = (
    ("h", 1), ("own",), ("g", 0, 0, 0), ("prep", 2), ("g", 0, 1, 0), ("h", 2),
    ("g", 1, 0, 0), ("g", 1, 1, 0), ("h", 3), ("g", 2, 0, 0), ("g", 0, 3, 0), ("prep", 0),
    ("prep", 3), ("h", 4), ("g", 2, 1, 0), ("tab",), ("g", 0, 2, 0), ("h", 5),
    ("g", 1, 3, 0), ("g", 3, 0, 0), ("g", 1, 2, 0), ("g", 3, 1, 0), ("pk", 3), ("pk", 1),
    ("pk", 0), ("g", 2, 3, 0), ("prep", 1), ("mu", 0), ("g", 2, 2, 0), ("g", 3, 3, 0),
    ("pk", 2), ("mc", 0), ("ma", 0), ("mu", 1), ("mc", 1), ("ma", 1),
    ("g", 3, 2, 0), ("mu", 3), ("mc", 3), ("s", 1, 0, 0), ("s", 1, 1, 0), ("ma", 3),
    ("mu", 2), ("mc", 2), ("ma", 2), ("s", 2, 0, 0), ("s", 2, 1, 0), ("add", 3),
    ("s", 1, 3, 0), ("s", 3, 0, 0), ("s", 1, 2, 0), ("add", 0), ("s", 3, 1, 0), ("add", 1),
    ("add", 2), ("t", 0), ("s", 2, 3, 0), ("s", 4, 1, 0), ("t", 1), ("s", 2, 2, 0),
    ("t", 2), ("s", 3, 3, 0), ("t", 3), ("s", 3, 2, 0), ("t", 4), ("s", 4, 3, 0),
    ("t", 5), ("s", 4, 2, 0), ("s", 4, 0, 0),
)
FAR = (0, 1, 3, 2)


def wrap(i, n):
    return lax.rem(i + n, n)


def kernel(
    tok_ref, ids_ref, logit_ref, gate_hbm, up_hbm, down_hbm, out_ref,
    gate_raw, up_raw, down_raw, gate_t, up_t, down_t,
    xa, pa, hidden, sel, w_high, w_low,
    disp_send, disp_recv, ret_send, ret_recv, a1, a2, a3, a4,
    meta, slots, mixes, sel_c, wc_high, wc_low,
    raw, xs, xc, pc, tr, acc, tsum, z1, z2, z3, z4, y1, y2,
    weight_sem, disp_ss, disp_rs, ret_ss, ret_rs, ss, rs, cs, cr, xss, xrs, tss, trs, local_sem,
):
    me = lax.axis_index("expert")
    place = lax.axis_index("split")
    x = me // 4
    zl = lax.rem(me // 2, 2)
    c = lax.rem(me, 2)
    z = place // 4
    y = lax.rem(place, 4)
    z8 = z * 2 + zl

    def at_z(zz):
        return (me, wrap(zz, 4) * 4 + y)

    def at_y(yy):
        return (me, z * 4 + wrap(yy, 4))

    def at_z8(zz):
        w = wrap(zz, 8)
        return (x * 4 + lax.rem(w, 2) * 2 + c, (w // 2) * 4 + y)

    def at_x(r, core):
        return (lax.rem(x + r, 4) * 4 + zl * 2 + core, place)

    def remote(src, dst, send, recv, dev):
        return pltpu.make_async_remote_copy(
            src_ref=src, dst_ref=dst, send_sem=send, recv_sem=recv, device_id=dev, device_id_type=MESH)

    barrier = pltpu.get_barrier_semaphore()
    for d in range(1, 16):
        pl.semaphore_signal(barrier, inc=1, device_id=(wrap(me + d, 16), place), device_id_type=MESH)
    for dev in (at_z(z + 1), at_z(z - 1), at_y(y + 1), at_y(y - 1), at_z8(z8 + 2 * zl - 1)):
        pl.semaphore_signal(barrier, inc=1, device_id=dev, device_id_type=MESH)

    loads = [
        pltpu.make_async_copy(src, dst, weight_sem.at[i])
        for i, (src, dst) in enumerate(((gate_hbm, gate_raw), (up_hbm, up_raw), (down_hbm, down_raw)))
    ]
    for load in loads:
        load.start()

    tok = tok_ref[...]
    raw[z8, y] = tok[RA:, :]
    meta[zl, 0:2, :] = ids_ref[...].astype(F32)
    meta[zl, 2:4, :] = logit_ref[...]
    meta[zl, 4:8, :] = jnp.zeros((4, 256), F32)

    def swap_meta():
        return remote(meta.at[zl], meta.at[zl], cs.at[24], cr.at[24], (x * 4 + (1 - zl) * 2 + c, place))

    def head(step, sign, arriving=False):
        lo = sign > 0
        k = step * 2 + (0 if lo else 1)
        back = -sign if arriving else 0
        if step == 0:
            ref = raw.at[z8, wrap(y + back, 4)]
        elif step == 1:
            ref = raw.at[z8, wrap(y - sign + back + 4, 4), pl.ds(0 if lo else HC, HC)]
        else:
            n = step - 2
            chunk = wrap(z8 - sign * n + back + 8, 8)
            ref = raw.at[chunk] if n < 3 else raw.at[chunk, pl.ds(0 if lo else 2, 2)]
        return remote(ref, ref, cs.at[k], cr.at[k], at_y(y + sign) if step < 2 else at_z8(z8 + sign))

    def head_step(step):
        for sign in (1, -1):
            head(step - 1, sign, True).wait_recv()
        for sign in (1, -1):
            head(step, sign).start()

    labels = lax.broadcasted_iota(jnp.int32, (16, 256), 0).astype(F32)
    earlier = lax.broadcasted_iota(jnp.int32, (256, 256), 0) < lax.broadcasted_iota(jnp.int32, (256, 256), 1)
    earlier = jnp.where(earlier, 1.0, 0.0).astype(BF16)
    sub = lax.broadcasted_iota(jnp.int32, (64, 256), 0).astype(F32)
    zero = jnp.zeros((64, 256), BF16)

    def slot_of(ids):
        hits = jnp.where((ids[0:1, :] == labels) | (ids[1:2, :] == labels), 1.0, 0.0)
        count = jnp.dot(hits.astype(BF16), earlier, preferred_element_type=F32)
        return jnp.where(hits > 0.5, count, -1.0)

    def mix_of(ids, logits):
        first = 1.0 / (1.0 + jnp.exp(logits[1:2, :] - logits[0:1, :]))
        return jnp.where(ids[0:1, :] == labels, first, jnp.where(ids[1:2, :] == labels, 1.0 - first, 0.0))

    ids = ids_ref[...].astype(F32)
    slot = slot_of(ids)
    mix = mix_of(ids, logit_ref[...])

    def one_hot(row):
        return jnp.where(sub == row, 1.0, 0.0).astype(BF16)

    def split(row, w):
        full = jnp.where(sub == row, w, 0.0)
        top = full.astype(BF16)
        return top, (full - top.astype(F32)).astype(BF16)

    def place_two(ref, base, first, second):
        ref[base:base + 64, 0:256] = first
        ref[base:base + 64, 256:512] = zero
        ref[base + 64:base + 128, 0:256] = zero
        ref[base + 64:base + 128, 256:512] = second

    for e in range(16):
        one = one_hot(slot[e:e + 1, :])
        place_two(sel, e * 128, one, one)

    pl.semaphore_wait(barrier, 20)
    swap_meta().start()
    for sign in (1, -1):
        head(0, sign).start()

    halves = jnp.concatenate([tok[0:HA, :], tok[HA:RA, :]], axis=1)
    for e in range(16):
        disp_send[e] = lax.dot_general(
            halves, sel[e * 128:e * 128 + 128, :], (((1,), (1,)), ((), ())), preferred_element_type=F32
        ).astype(BF16)
    disp_recv[pl.ds(me, 1)] = disp_send[pl.ds(me, 1)]

    def dispatch(d):
        step, inner = d // 4, d % 4
        target = wrap(x + FAR[step], 4) * 4 + wrap(me - x * 4 + inner, 4)
        return remote(disp_send.at[target], disp_recv.at[me], disp_ss.at[d], disp_rs.at[me], (target, place))

    for d in range(1, 16):
        dispatch(d).start()

    def tables():
        remote(meta.at[zl], meta.at[1 - zl], cs.at[24], cr.at[24], (x * 4 + (1 - zl) * 2 + c, place)).wait_recv()
        for b in (0, 1):
            both = meta[b]
            slots[b] = slot_of(both[0:2])
            mixes[b] = mix_of(both[0:2], both[2:4])
        for r in range(4):
            for core in (0, 1):
                e = lax.rem(x + r, 4) * 4 + zl * 2 + core
                base = r * 256 + core * 128
                row = [slots[b, pl.ds(e, 1), :] for b in (0, 1)]
                w = [mixes[b, pl.ds(e, 1), :] for b in (0, 1)]
                place_two(sel_c, base, one_hot(row[0]), one_hot(row[1]))
                first, second = split(row[0], w[0]), split(row[1], w[1])
                place_two(wc_high, base, first[0], second[0])
                place_two(wc_low, base, first[1], second[1])

    def own_weights():
        for e in range(16):
            top, rest = split(slot[e:e + 1, :], mix[e:e + 1, :])
            place_two(w_high, e * 128, top, top)
            place_two(w_low, e * 128, rest, rest)

    def x_out(r, core):
        return remote(xs.at[r, core], xc.at[(4 - r) % 4, c], xss.at[r, core], xrs.at[(4 - r) % 4, c], at_x(r, core))

    def x_back(r, core):
        return remote(pc.at[r, core], tr.at[(4 - r) % 4, c], tss.at[r, core], trs.at[(4 - r) % 4, c], at_x(r, core))

    def keep(out):
        src, dst, i = (xs.at[0, c], xc.at[0, c], 0) if out else (pc.at[0, c], tr.at[0, c], 1)
        return pltpu.make_async_copy(src, dst, local_sem.at[i])

    def x_arrived(refs, sems, r, core):
        remote(refs.at[r, core], refs.at[r, core], xss.at[0, 0], sems.at[r, core], at_x(r, core)).wait_recv()

    def pick_slots(r):
        base = r * 256

        @pl.loop(0, 4)
        def _(i):
            first = raw[i * 2].reshape(4 * RC, 256)
            second = raw[i * 2 + 1].reshape(4 * RC, 256)
            got = lax.dot_general(
                first, sel_c[base:base + 256, 0:256], (((1,), (1,)), ((), ())), preferred_element_type=F32)
            got = got + lax.dot_general(
                second, sel_c[base:base + 256, 256:512], (((1,), (1,)), ((), ())), preferred_element_type=F32)
            got = got.astype(BF16)
            s = pl.ds(i * 4, 4)
            xs[r, 0, s] = got[:, :128].reshape(4, RC, 128)
            xs[r, 1, s] = got[:, 128:].reshape(4, RC, 128)

        if r == 0:
            keep(True).start()
            x_out(0, 1 - c).start()
        else:
            for core in (0, 1):
                x_out(r, core).start()

    def wait_slots(r):
        if r == 0:
            keep(True).wait()
            x_arrived(xc, xrs, 0, 1 - c)
        else:
            for core in (0, 1):
                x_arrived(xc, xrs, r, core)

    def add_up(r, first, last):
        if r == 0:
            keep(False).wait()
            x_arrived(tr, trs, 0, 1 - c)
        else:
            for core in (0, 1):
                x_arrived(tr, trs, r, core)

        @pl.loop(0, 4)
        def _(i):
            s = pl.ds(i * 4, 4)
            rows = jnp.concatenate(
                [tr[r, 0, s].reshape(4 * RC, 128), tr[r, 1, s].reshape(4 * RC, 128)], axis=1)
            base = r * 256
            total = jnp.dot(rows, wc_high[base:base + 256, :], preferred_element_type=F32)
            total = total + jnp.dot(rows, wc_low[base:base + 256, :], preferred_element_type=F32)
            if not first:
                total = total + acc[i]
            if last:
                total = total.astype(BF16)
                tsum[i * 2] = total[:, 0:256].reshape(4, RC, 256)
                tsum[i * 2 + 1] = total[:, 256:512].reshape(4, RC, 256)
            else:
                acc[i] = total

    def add_into(ref, *others):
        total = ref[...].astype(F32)
        for o in others:
            total = total + o[...].astype(F32)
        ref[...] = total.astype(BF16)

    tail_land = (z1, z2, z3, z4, y1, y2)

    def tail(step, sign):
        lo = sign > 0
        side = 0 if lo else 1
        k = 12 + step * 2 + side
        if step == 0:
            src = tsum.at[wrap(z8 + 4, 8), pl.ds(0 if lo else 2, 2)]
        elif step < 4:
            src = tsum.at[wrap(z8 + sign * (4 - step), 8)]
        elif step == 4:
            src = tsum.at[z8, wrap(y + 2, 4), pl.ds(0 if lo else HC, HC)]
        else:
            src = tsum.at[z8, wrap(y + sign, 4)]
        return remote(src, tail_land[step].at[side], cs.at[k], cr.at[k],
                      at_z8(z8 + sign) if step < 4 else at_y(y + sign))

    def tail_step(step):
        if step > 0:
            for sign in (1, -1):
                tail(step - 1, sign).wait_recv()
        got = tail_land[step - 1]
        if step == 1:
            add_into(tsum.at[wrap(z8 + 3, 8), pl.ds(0, 2)], got.at[0])
            add_into(tsum.at[wrap(z8 - 3, 8), pl.ds(2, 2)], got.at[1])
        elif step in (2, 3):
            add_into(tsum.at[wrap(z8 + 4 - step, 8)], got.at[0])
            add_into(tsum.at[wrap(z8 - 4 + step, 8)], got.at[1])
        elif step == 4:
            add_into(tsum.at[z8], got.at[0], got.at[1])
        elif step == 5:
            add_into(tsum.at[z8, wrap(y + 1, 4), pl.ds(0, HC)], got.at[0])
            add_into(tsum.at[z8, wrap(y - 1, 4), pl.ds(HC, HC)], got.at[1])
        for sign in (1, -1):
            tail(step, sign).start()

    land = ((a1, a2, a3, a4),)

    def at_part(ref, r, part, i, j, half=None):
        r0, n = PARTS[part]
        zi, yi = (i, j) if part == 0 else (j, i)
        if half is None:
            return ref.at[r, zi, yi, pl.ds(r0, n)]
        if n % 32 == 0:
            return ref.at[r, zi, yi, pl.ds(r0 + half * (n // 2), n // 2)]
        return ref.at[r, zi, yi, pl.ds(r0, n), pl.ds(half * 128, 128)]

    def coords(part):
        return (z, y) if part == 0 else (y, z)

    def device(part, axis, i):
        return at_z(i) if axis == part else at_y(i)

    ALL, LOW, HIGH = pl.ds(0, 4), pl.ds(0, 2), pl.ds(2, 2)

    def gather(part, step, sign, r, arriving=False):
        u, v = coords(part)
        back = -sign if arriving else 0
        lo = sign > 0
        if step == 0:
            ref = at_part(xa, r, part, wrap(u + back, 4), v)
        elif step == 1:
            ref = at_part(xa, r, part, wrap(u - sign + back + 4, 4), v, 0 if lo else 1)
        elif step == 2:
            ref = at_part(xa, r, part, ALL, wrap(v + back, 4))
        else:
            ref = at_part(xa, r, part, LOW if lo else HIGH, wrap(v - sign + back + 4, 4))
        k = step * 2 + (0 if lo else 1)
        axis = 0 if step < 2 else 1
        return remote(ref, ref, ss.at[r, part, k], rs.at[r, part, k],
                      device(part, axis, (u if axis == 0 else v) + sign))

    def scatter(part, step, sign, r):
        u, v = coords(part)
        lo = sign > 0
        side = 0 if lo else 1
        if step == 0:
            src = at_part(pa, r, part, LOW if lo else HIGH, wrap(v + 2, 4))
        elif step == 1:
            src = at_part(pa, r, part, ALL, wrap(v + sign, 4))
        elif step == 2:
            src = at_part(pa, r, part, wrap(u + 2, 4), v, side)
        else:
            src = at_part(pa, r, part, wrap(u + sign, 4), v)
        k = 8 + step * 2 + side
        axis = 1 if step < 2 else 0
        return remote(src, land[part][step].at[r, side], ss.at[r, part, k], rs.at[r, part, k],
                      device(part, axis, (u if axis == 0 else v) + sign))

    def block_of(r, core, b):
        return lax.rem(x + r, 4) * 4 + b * 2 + core

    def arrive(r):
        for core in (0, 1):
            for b in (0, 1):
                src = block_of(r, core, b)

                @pl.when(src != me)
                def _():
                    remote(disp_recv.at[src], disp_recv.at[src], disp_ss.at[0], disp_rs.at[src],
                           (src, place)).wait_recv()
            one, two = disp_recv[block_of(r, core, 0)], disp_recv[block_of(r, core, 1)]
            lanes = slice(core * 128, core * 128 + 128)
            xa[r, z, y, 0:HA, lanes] = jnp.concatenate([one[:, :64], two[:, :64]], axis=1)
            xa[r, z, y, HA:RA, lanes] = jnp.concatenate([one[:, 64:], two[:, 64:]], axis=1)

    def units(r):
        for part in range(len(PARTS)):
            for sign in (1, -1):
                gather(part, 3, sign, r, True).wait_recv()
        wait_slots(r)
        rows = xa[r].reshape(16 * RA, COLS)
        more = jnp.concatenate([xc[r, 0].reshape(16 * RC, 128), xc[r, 1].reshape(16 * RC, 128)], axis=1)

        @pl.loop(0, 2)
        def _(i):
            m = pl.ds(pl.multiple_of(i * 256, 256), 256)

            def product(w):
                return jnp.dot(w[m, 0:16 * RA], rows, preferred_element_type=F32) + jnp.dot(
                    w[m, 16 * RA:], more, preferred_element_type=F32)

            gate, up = product(gate_t), product(up_t)
            hidden[m, :] = (gate / (1.0 + jnp.exp(-gate)) * up).astype(BF16)

    def results_c(r):
        @pl.loop(0, 2)
        def _(i):
            m = pl.ds(pl.multiple_of(16 * RA + i * 8 * RC, 128), 8 * RC)
            part = jnp.dot(down_t[m, :], hidden[...], preferred_element_type=F32).astype(BF16)
            s = pl.ds(i * 8, 8)
            pc[r, 0, s] = part[:, :128].reshape(8, RC, 128)
            pc[r, 1, s] = part[:, 128:].reshape(8, RC, 128)

        if r == 0:
            keep(False).start()
            x_back(0, 1 - c).start()
        else:
            for core in (0, 1):
                x_back(r, core).start()

    def results_a(r):
        @pl.loop(0, 4)
        def _(i):
            m = pl.ds(pl.multiple_of(i * 4 * RA, 128), 4 * RA)
            part = jnp.dot(down_t[m, :], hidden[...], preferred_element_type=F32)
            pa[r, i] = part.astype(BF16).reshape(4, RA, COLS)

        for part in range(len(PARTS)):
            for sign in (1, -1):
                scatter(part, 0, sign, r).start()

    def returning(r, core, b):
        target = block_of(r, core, b)
        return remote(ret_send.at[r, core, b], ret_recv.at[me], ret_ss.at[r, core, b], ret_rs.at[me], (target, place))

    def give_back(r):
        rows = []
        for part, (r0, n) in enumerate(PARTS):
            last = land[part][3]
            total = pa[r, z, y, r0:r0 + n].astype(F32) + last[r, 0].astype(F32) + last[r, 1].astype(F32)
            rows.append(total.astype(BF16))
        whole = jnp.concatenate(rows, axis=0)
        for core in (0, 1):
            tile = whole[:, core * 128:core * 128 + 128]
            for b in (0, 1):
                lanes = slice(b * 64, b * 64 + 64)
                ret_send[r, core, b] = jnp.concatenate([tile[0:HA, lanes], tile[HA:RA, lanes]], axis=1)

                @pl.when(block_of(r, core, b) != me)
                def _():
                    returning(r, core, b).start()

                @pl.when(block_of(r, core, b) == me)
                def _():
                    ret_recv[pl.ds(me, 1)] = ret_send[r, core, pl.ds(b, 1)]

    def gather_op(step, r, part):
        if step == 0:
            if ("here", r) not in seen:
                seen.add(("here", r))
                arrive(r)
        else:
            for sign in (1, -1):
                gather(part, step - 1, sign, r, True).wait_recv()
        for sign in (1, -1):
            gather(part, step, sign, r).start()

    def scatter_op(step, r, part):
        for sign in (1, -1):
            scatter(part, step - 1, sign, r).wait_recv()
        if step == 4:
            seen.add(("summed", r, part))
            if all(("summed", r, p) in seen for p in range(len(PARTS))):
                give_back(r)
            return
        u, v = coords(part)
        got = land[part][step - 1]
        if step == 1:
            add_into(at_part(pa, r, part, LOW, wrap(v + 1, 4)), got.at[r, 0])
            add_into(at_part(pa, r, part, HIGH, wrap(v - 1, 4)), got.at[r, 1])
        elif step == 2:
            add_into(at_part(pa, r, part, ALL, v), got.at[r, 0], got.at[r, 1])
        else:
            add_into(at_part(pa, r, part, wrap(u + 1, 4), v, 0), got.at[r, 0])
            add_into(at_part(pa, r, part, wrap(u - 1, 4), v, 1), got.at[r, 1])
        for sign in (1, -1):
            scatter(part, step, sign, r).start()

    def prepare(i):
        m = pl.ds(pl.multiple_of(i * 768, 128), 768)
        wide = pl.ds(pl.multiple_of(i * 4 * RA, 128), 4 * RA)
        thin = pl.ds(pl.multiple_of(16 * RA + i * 4 * RC, 128), 4 * RC)

        def sorted_rows(w):
            return (jnp.concatenate([w[n * 192:n * 192 + RA] for n in range(4)], axis=0),
                    jnp.concatenate([w[n * 192 + RA:n * 192 + 192] for n in range(4)], axis=0))

        for src, dst in ((gate_raw, gate_t), (up_raw, up_t)):
            first, second = sorted_rows(src[m, :])
            dst[:, wide] = first.T
            dst[:, thin] = second.T
        first, second = sorted_rows(down_raw[:, m].T)
        down_t[wide, :] = first
        down_t[thin, :] = second

    def gather_sent():
        swap_meta().wait_send()
        for sign in (1, -1):
            for step in range(6):
                head(step, sign).wait_send()
        x_out(0, 1 - c).wait_send()
        for r in (1, 2, 3):
            for core in (0, 1):
                x_out(r, core).wait_send()
        for d in range(1, 16):
            dispatch(d).wait_send()
        for r in range(GROUPS):
            for part in range(len(PARTS)):
                for sign in (1, -1):
                    for step in range(4):
                        gather(part, step, sign, r).wait_send()

    def sums_sent():
        for sign in (1, -1):
            for step in range(5):
                tail(step, sign).wait_send()
        x_back(0, 1 - c).wait_send()
        for r in (1, 2, 3):
            for core in (0, 1):
                x_back(r, core).wait_send()
        for r in range(GROUPS):
            for part in range(len(PARTS)):
                for sign in (1, -1):
                    for step in range(4):
                        scatter(part, step, sign, r).wait_send()

    seen = set()

    def loaded():
        if "loaded" not in seen:
            seen.add("loaded")
            for load in loads:
                load.wait()

    for op, *at in ORDER:
        if op == "h":
            head_step(*at)
        elif op == "pk":
            if "tokens" not in seen:
                seen.add("tokens")
                for sign in (1, -1):
                    head(5, sign, True).wait_recv()
            pick_slots(*at)
        elif op == "g":
            gather_op(*at)
        elif op == "mu":
            units(*at)
        elif op == "mc":
            results_c(*at)
        elif op == "ma":
            results_a(*at)
        elif op == "s":
            scatter_op(*at)
        elif op == "add":
            added = sum(1 for k in seen if k[0] == "add")
            seen.add(("add", *at))
            add_up(*at, added == 0, added == 3)
        elif op == "t":
            tail_step(*at)
            if at[0] == 2:
                gather_sent()
        elif op == "prep":
            loaded()
            prepare(at[0])
        elif op == "tab":
            tables()
        elif op == "own":
            own_weights()

    sums_sent()
    for d in range(1, 16):
        src = wrap(me + d, 16)
        remote(ret_recv.at[src], ret_recv.at[src], disp_ss.at[0], ret_rs.at[src], (src, place)).wait_recv()
    back = jnp.concatenate([ret_recv[e] for e in range(16)], axis=1)
    mixed = jnp.dot(back, w_high[...], preferred_element_type=F32) + jnp.dot(
        back, w_low[...], preferred_element_type=F32)
    out_ref[0:HA, :] = mixed[:, 0:256].astype(BF16)
    out_ref[HA:RA, :] = mixed[:, 256:512].astype(BF16)

    for sign in (1, -1):
        tail(5, sign).wait_recv()
    out_ref[RA:, :] = (tsum[z8, y].astype(F32) + y2[0].astype(F32) + y2[1].astype(F32)).astype(BF16)

    for sign in (1, -1):
        tail(5, sign).wait_send()
    for r in range(GROUPS):
        for core in (0, 1):
            for b in (0, 1):
                @pl.when(block_of(r, core, b) != me)
                def _():
                    returning(r, core, b).wait_send()


def body(tokens, expert_ids, pair_logits, gate_weight, up_weight, down_weight):
    vmem = pl.BlockSpec(memory_space=pltpu.VMEM)
    hbm = pl.BlockSpec(memory_space=pl.ANY)
    dma = pltpu.SemaphoreType.DMA

    def buf(*shape):
        return pltpu.VMEM(shape, BF16)

    def buf32(*shape):
        return pltpu.VMEM(shape, F32)

    landing = []
    for _, n in PARTS:
        half = (n // 2, COLS) if n % 32 == 0 else (n, 128)
        landing += [
            buf(GROUPS, 2, 2, n, COLS), buf(GROUPS, 2, 4, n, COLS), buf(GROUPS, 2, *half), buf(GROUPS, 2, n, COLS)]
    out = pl.pallas_call(
        kernel,
        out_shape=jax.ShapeDtypeStruct((192, 256), BF16),
        in_specs=[vmem, vmem, vmem, hbm, hbm, hbm],
        out_specs=vmem,
        scratch_shapes=[
            buf(3072, 512), buf(3072, 512), buf(512, 3072),
            buf(512, 3072), buf(512, 3072), buf(3072, 512),
            buf(GROUPS, 4, 4, RA, COLS), buf(GROUPS, 4, 4, RA, COLS), buf(512, COLS),
            buf(2048, 512), buf(2048, 512), buf(2048, 512),
            buf(16, HA, 128), buf(16, HA, 128), buf(GROUPS, 2, 2, HA, 128), buf(16, HA, 128),
            *landing,
            buf32(2, 8, 256), buf32(2, 16, 256), buf32(2, 16, 256),
            buf(1024, 512), buf(1024, 512), buf(1024, 512),
            buf(8, 4, RC, 256), buf(4, 2, 16, RC, 128), buf(4, 2, 16, RC, 128),
            buf(4, 2, 16, RC, 128), buf(4, 2, 16, RC, 128),
            buf32(4, 4 * RC, 512), buf(8, 4, RC, 256),
            buf(2, 2, RC, 256), buf(2, 4, RC, 256), buf(2, 4, RC, 256), buf(2, 4, RC, 256),
            buf(2, HC, 256), buf(2, RC, 256),
            dma((3,)), dma((16,)), dma((16,)), dma((GROUPS, 2, 2)), dma((16,)),
            dma((GROUPS, len(PARTS), 16)), dma((GROUPS, len(PARTS), 16)), dma((25,)), dma((25,)),
            dma((4, 2)), dma((4, 2)), dma((4, 2)), dma((4, 2)), dma((2,)),
        ],
        compiler_params=pltpu.CompilerParams(
            collective_id=0, has_side_effects=True, vmem_limit_bytes=60 * 2**20),
        cost_estimate=pl.CostEstimate(flops=9_700_000_000, bytes_accessed=10_000_000, transcendentals=524288),
    )(tokens.T, expert_ids.T, pair_logits.T, gate_weight[0], up_weight[0], down_weight[0])
    return out.T


def solution(mesh):
    in_specs = (
        P("expert", "split"),
        P("expert", None),
        P("expert", None),
        P("expert", None, "split"),
        P("expert", None, "split"),
        P("expert", "split", None),
    )
    return jax.shard_map(body, mesh=mesh, in_specs=in_specs, out_specs=P("expert", "split"), check_vma=False)
```

```python
import functools

import jax
import jax.numpy as jnp
from jax import lax
from jax.experimental import pallas as pl
from jax.experimental.pallas import tpu as pltpu
from jax.sharding import PartitionSpec as P

MESH = pl.DeviceIdType.MESH
BF16 = jnp.bfloat16
F32 = jnp.float32

COLS = 256
GROUPS = 4
PARTS = ((0, 128), (128, 32))
RA = 160
RC = 32
HA, HC = RA // 2, RC // 2
ORDER = (
    ("tab",), ("prep", 0), ("h", 1), ("g", 0, 0, 0), ("g", 0, 1, 1), ("g", 0, 2, 0),
    ("g", 0, 0, 1), ("g", 1, 0, 1), ("g", 1, 0, 0), ("g", 0, 2, 1), ("prep", 1), ("h", 2),
    ("g", 0, 1, 0), ("g", 2, 0, 0), ("g", 1, 2, 0), ("h", 3), ("g", 0, 3, 1), ("g", 1, 1, 0),
    ("g", 0, 3, 0), ("g", 2, 2, 0), ("h", 4), ("g", 1, 3, 1), ("g", 1, 1, 1), ("g", 2, 0, 1),
    ("g", 1, 2, 1), ("g", 3, 0, 0), ("h", 5), ("prep", 3), ("g", 2, 1, 0), ("g", 1, 3, 0),
    ("prep", 2), ("g", 3, 0, 1), ("pk", 0), ("pk", 2), ("g", 2, 1, 1), ("pk", 3),
    ("g", 2, 3, 0), ("pk", 1), ("g", 2, 3, 1), ("mu", 0), ("g", 3, 1, 1), ("mc", 0),
    ("g", 2, 2, 1), ("g", 3, 1, 0), ("g", 3, 3, 0), ("g", 3, 3, 1), ("ma", 0), ("add", 0),
    ("mu", 1), ("g", 3, 2, 0), ("mc", 1), ("ma", 1), ("mu", 3), ("g", 3, 2, 1),
    ("mc", 3), ("s", 1, 0, 1), ("ma", 3), ("s", 1, 1, 0), ("s", 1, 1, 1), ("mu", 2),
    ("mc", 2), ("add", 1), ("s", 1, 0, 0), ("s", 1, 3, 1), ("s", 2, 1, 0), ("ma", 2),
    ("add", 3), ("s", 1, 3, 0), ("own",), ("add", 2), ("t", 0), ("s", 2, 0, 1),
    ("s", 2, 1, 1), ("s", 3, 1, 0), ("t", 1), ("s", 2, 3, 1), ("s", 1, 2, 1), ("s", 1, 2, 0),
    ("t", 2), ("s", 3, 3, 1), ("s", 2, 3, 0), ("s", 3, 1, 1), ("s", 2, 2, 1), ("s", 2, 0, 0),
    ("t", 3), ("s", 3, 0, 1), ("s", 3, 3, 0), ("s", 2, 2, 0), ("s", 3, 2, 1), ("s", 4, 3, 1),
    ("s", 4, 2, 1), ("s", 3, 0, 0), ("s", 4, 1, 1), ("t", 4), ("s", 3, 2, 0), ("s", 4, 0, 0),
    ("s", 4, 1, 0), ("s", 4, 0, 1), ("s", 4, 3, 0), ("s", 4, 2, 0), ("t", 5),
)
FAR = (0, 1, 3, 2)


def wrap(i, n):
    return lax.rem(i + n, n)


def kernel(
    tok_ref, ids_ref, logit_ref, gate_hbm, up_hbm, down_hbm, out_ref,
    gate_raw, up_raw, down_raw, gate_t, up_t, down_t,
    xa, pa, hidden, sel, w_high, w_low,
    disp_send, disp_recv, ret_send, ret_recv, a1, a2, a3, a4, b1, b2, b3, b4,
    meta, slots, mixes, sel_c, wc_high, wc_low,
    raw, xs, xc, pc, tr, acc, tsum, z1, z2, z3, z4, y1, y2,
    weight_sem, disp_ss, disp_rs, ret_ss, ret_rs, ss, rs, cs, cr, xss, xrs, tss, trs, local_sem,
):
    me = lax.axis_index("expert")
    place = lax.axis_index("split")
    x = me // 4
    zl = lax.rem(me // 2, 2)
    c = lax.rem(me, 2)
    z = place // 4
    y = lax.rem(place, 4)
    z8 = z * 2 + zl

    def at_z(zz):
        return (me, wrap(zz, 4) * 4 + y)

    def at_y(yy):
        return (me, z * 4 + wrap(yy, 4))

    def at_z8(zz):
        w = wrap(zz, 8)
        return (x * 4 + lax.rem(w, 2) * 2 + c, (w // 2) * 4 + y)

    def at_x(r, core):
        return (lax.rem(x + r, 4) * 4 + zl * 2 + core, place)

    def remote(src, dst, send, recv, dev):
        return pltpu.make_async_remote_copy(
            src_ref=src, dst_ref=dst, send_sem=send, recv_sem=recv, device_id=dev, device_id_type=MESH)

    barrier = pltpu.get_barrier_semaphore()
    for d in range(1, 16):
        pl.semaphore_signal(barrier, inc=1, device_id=(wrap(me + d, 16), place), device_id_type=MESH)
    for dev in (at_z(z + 1), at_z(z - 1), at_y(y + 1), at_y(y - 1), at_z8(z8 + 2 * zl - 1)):
        pl.semaphore_signal(barrier, inc=1, device_id=dev, device_id_type=MESH)

    loads = [
        pltpu.make_async_copy(src, dst, weight_sem.at[i])
        for i, (src, dst) in enumerate(((gate_hbm, gate_raw), (up_hbm, up_raw), (down_hbm, down_raw)))
    ]
    for load in loads:
        load.start()

    tok = tok_ref[...]
    raw[z8, y] = tok[RA:, :]
    meta[zl, 0:2, :] = ids_ref[...].astype(F32)
    meta[zl, 2:4, :] = logit_ref[...]
    meta[zl, 4:8, :] = jnp.zeros((4, 256), F32)

    def swap_meta():
        return remote(meta.at[zl], meta.at[zl], cs.at[24], cr.at[24], (x * 4 + (1 - zl) * 2 + c, place))

    def head(step, sign, arriving=False):
        lo = sign > 0
        k = step * 2 + (0 if lo else 1)
        back = -sign if arriving else 0
        if step == 0:
            ref = raw.at[z8, wrap(y + back, 4)]
        elif step == 1:
            ref = raw.at[z8, wrap(y - sign + back + 4, 4), pl.ds(0 if lo else HC, HC)]
        else:
            n = step - 2
            chunk = wrap(z8 - sign * n + back + 8, 8)
            ref = raw.at[chunk] if n < 3 else raw.at[chunk, pl.ds(0 if lo else 2, 2)]
        return remote(ref, ref, cs.at[k], cr.at[k], at_y(y + sign) if step < 2 else at_z8(z8 + sign))

    def head_step(step):
        for sign in (1, -1):
            head(step - 1, sign, True).wait_recv()
        for sign in (1, -1):
            head(step, sign).start()

    labels = lax.broadcasted_iota(jnp.int32, (16, 256), 0).astype(F32)
    earlier = lax.broadcasted_iota(jnp.int32, (256, 256), 0) < lax.broadcasted_iota(jnp.int32, (256, 256), 1)
    earlier = jnp.where(earlier, 1.0, 0.0).astype(BF16)
    sub = lax.broadcasted_iota(jnp.int32, (64, 256), 0).astype(F32)
    zero = jnp.zeros((64, 256), BF16)

    def slot_of(ids):
        hits = jnp.where((ids[0:1, :] == labels) | (ids[1:2, :] == labels), 1.0, 0.0)
        count = jnp.dot(hits.astype(BF16), earlier, preferred_element_type=F32)
        return jnp.where(hits > 0.5, count, -1.0)

    def mix_of(ids, logits):
        first = 1.0 / (1.0 + jnp.exp(logits[1:2, :] - logits[0:1, :]))
        return jnp.where(ids[0:1, :] == labels, first, jnp.where(ids[1:2, :] == labels, 1.0 - first, 0.0))

    ids = ids_ref[...].astype(F32)
    slot = slot_of(ids)
    mix = mix_of(ids, logit_ref[...])

    def one_hot(row):
        return jnp.where(sub == row, 1.0, 0.0).astype(BF16)

    def split(row, w):
        full = jnp.where(sub == row, w, 0.0)
        top = full.astype(BF16)
        return top, (full - top.astype(F32)).astype(BF16)

    def place_two(ref, base, first, second):
        ref[base:base + 64, 0:256] = first
        ref[base:base + 64, 256:512] = zero
        ref[base + 64:base + 128, 0:256] = zero
        ref[base + 64:base + 128, 256:512] = second

    for e in range(16):
        one = one_hot(slot[e:e + 1, :])
        place_two(sel, e * 128, one, one)

    pl.semaphore_wait(barrier, 20)
    swap_meta().start()
    for sign in (1, -1):
        head(0, sign).start()

    halves = jnp.concatenate([tok[0:HA, :], tok[HA:RA, :]], axis=1)
    for e in range(16):
        disp_send[e] = lax.dot_general(
            halves, sel[e * 128:e * 128 + 128, :], (((1,), (1,)), ((), ())), preferred_element_type=F32
        ).astype(BF16)
    disp_recv[pl.ds(me, 1)] = disp_send[pl.ds(me, 1)]

    def dispatch(d):
        step, inner = d // 4, d % 4
        target = wrap(x + FAR[step], 4) * 4 + wrap(me - x * 4 + inner, 4)
        return remote(disp_send.at[target], disp_recv.at[me], disp_ss.at[d], disp_rs.at[me], (target, place))

    for d in range(1, 16):
        dispatch(d).start()

    def tables():
        remote(meta.at[zl], meta.at[1 - zl], cs.at[24], cr.at[24], (x * 4 + (1 - zl) * 2 + c, place)).wait_recv()
        for b in (0, 1):
            both = meta[b]
            slots[b] = slot_of(both[0:2])
            mixes[b] = mix_of(both[0:2], both[2:4])
        for r in range(4):
            for core in (0, 1):
                e = lax.rem(x + r, 4) * 4 + zl * 2 + core
                base = r * 256 + core * 128
                row = [slots[b, pl.ds(e, 1), :] for b in (0, 1)]
                w = [mixes[b, pl.ds(e, 1), :] for b in (0, 1)]
                place_two(sel_c, base, one_hot(row[0]), one_hot(row[1]))
                first, second = split(row[0], w[0]), split(row[1], w[1])
                place_two(wc_high, base, first[0], second[0])
                place_two(wc_low, base, first[1], second[1])

    def own_weights():
        for e in range(16):
            top, rest = split(slot[e:e + 1, :], mix[e:e + 1, :])
            place_two(w_high, e * 128, top, top)
            place_two(w_low, e * 128, rest, rest)

    def x_out(r, core):
        return remote(xs.at[r, core], xc.at[(4 - r) % 4, c], xss.at[r, core], xrs.at[(4 - r) % 4, c], at_x(r, core))

    def x_back(r, core):
        return remote(pc.at[r, core], tr.at[(4 - r) % 4, c], tss.at[r, core], trs.at[(4 - r) % 4, c], at_x(r, core))

    def keep(out):
        src, dst, i = (xs.at[0, c], xc.at[0, c], 0) if out else (pc.at[0, c], tr.at[0, c], 1)
        return pltpu.make_async_copy(src, dst, local_sem.at[i])

    def x_arrived(refs, sems, r, core):
        remote(refs.at[r, core], refs.at[r, core], xss.at[0, 0], sems.at[r, core], at_x(r, core)).wait_recv()

    def pick_slots(r):
        base = r * 256

        @pl.loop(0, 4)
        def _(i):
            first = raw[i * 2].reshape(4 * RC, 256)
            second = raw[i * 2 + 1].reshape(4 * RC, 256)
            got = lax.dot_general(
                first, sel_c[base:base + 256, 0:256], (((1,), (1,)), ((), ())), preferred_element_type=F32)
            got = got + lax.dot_general(
                second, sel_c[base:base + 256, 256:512], (((1,), (1,)), ((), ())), preferred_element_type=F32)
            got = got.astype(BF16)
            s = pl.ds(i * 4, 4)
            xs[r, 0, s] = got[:, :128].reshape(4, RC, 128)
            xs[r, 1, s] = got[:, 128:].reshape(4, RC, 128)

        if r == 0:
            keep(True).start()
            x_out(0, 1 - c).start()
        else:
            for core in (0, 1):
                x_out(r, core).start()

    def wait_slots(r):
        if r == 0:
            keep(True).wait()
            x_arrived(xc, xrs, 0, 1 - c)
        else:
            for core in (0, 1):
                x_arrived(xc, xrs, r, core)

    def add_up(r, first, last):
        if r == 0:
            keep(False).wait()
            x_arrived(tr, trs, 0, 1 - c)
        else:
            for core in (0, 1):
                x_arrived(tr, trs, r, core)

        @pl.loop(0, 4)
        def _(i):
            s = pl.ds(i * 4, 4)
            rows = jnp.concatenate(
                [tr[r, 0, s].reshape(4 * RC, 128), tr[r, 1, s].reshape(4 * RC, 128)], axis=1)
            base = r * 256
            total = jnp.dot(rows, wc_high[base:base + 256, :], preferred_element_type=F32)
            total = total + jnp.dot(rows, wc_low[base:base + 256, :], preferred_element_type=F32)
            if not first:
                total = total + acc[i]
            if last:
                total = total.astype(BF16)
                tsum[i * 2] = total[:, 0:256].reshape(4, RC, 256)
                tsum[i * 2 + 1] = total[:, 256:512].reshape(4, RC, 256)
            else:
                acc[i] = total

    def add_into(ref, *others):
        total = ref[...].astype(F32)
        for o in others:
            total = total + o[...].astype(F32)
        ref[...] = total.astype(BF16)

    tail_land = (z1, z2, z3, z4, y1, y2)

    def tail(step, sign):
        lo = sign > 0
        side = 0 if lo else 1
        k = 12 + step * 2 + side
        if step == 0:
            src = tsum.at[wrap(z8 + 4, 8), pl.ds(0 if lo else 2, 2)]
        elif step < 4:
            src = tsum.at[wrap(z8 + sign * (4 - step), 8)]
        elif step == 4:
            src = tsum.at[z8, wrap(y + 2, 4), pl.ds(0 if lo else HC, HC)]
        else:
            src = tsum.at[z8, wrap(y + sign, 4)]
        return remote(src, tail_land[step].at[side], cs.at[k], cr.at[k],
                      at_z8(z8 + sign) if step < 4 else at_y(y + sign))

    def tail_step(step):
        if step > 0:
            for sign in (1, -1):
                tail(step - 1, sign).wait_recv()
        got = tail_land[step - 1]
        if step == 1:
            add_into(tsum.at[wrap(z8 + 3, 8), pl.ds(0, 2)], got.at[0])
            add_into(tsum.at[wrap(z8 - 3, 8), pl.ds(2, 2)], got.at[1])
        elif step in (2, 3):
            add_into(tsum.at[wrap(z8 + 4 - step, 8)], got.at[0])
            add_into(tsum.at[wrap(z8 - 4 + step, 8)], got.at[1])
        elif step == 4:
            add_into(tsum.at[z8], got.at[0], got.at[1])
        elif step == 5:
            add_into(tsum.at[z8, wrap(y + 1, 4), pl.ds(0, HC)], got.at[0])
            add_into(tsum.at[z8, wrap(y - 1, 4), pl.ds(HC, HC)], got.at[1])
        for sign in (1, -1):
            tail(step, sign).start()

    land = ((a1, a2, a3, a4), (b1, b2, b3, b4))

    def at_part(ref, r, part, i, j, half=None):
        r0, n = PARTS[part]
        zi, yi = (i, j) if part == 0 else (j, i)
        if half is None:
            return ref.at[r, zi, yi, pl.ds(r0, n)]
        if n % 32 == 0:
            return ref.at[r, zi, yi, pl.ds(r0 + half * (n // 2), n // 2)]
        return ref.at[r, zi, yi, pl.ds(r0, n), pl.ds(half * 128, 128)]

    def coords(part):
        return (z, y) if part == 0 else (y, z)

    def device(part, axis, i):
        return at_z(i) if axis == part else at_y(i)

    ALL, LOW, HIGH = pl.ds(0, 4), pl.ds(0, 2), pl.ds(2, 2)

    def gather(part, step, sign, r, arriving=False):
        u, v = coords(part)
        back = -sign if arriving else 0
        lo = sign > 0
        if step == 0:
            ref = at_part(xa, r, part, wrap(u + back, 4), v)
        elif step == 1:
            ref = at_part(xa, r, part, wrap(u - sign + back + 4, 4), v, 0 if lo else 1)
        elif step == 2:
            ref = at_part(xa, r, part, ALL, wrap(v + back, 4))
        else:
            ref = at_part(xa, r, part, LOW if lo else HIGH, wrap(v - sign + back + 4, 4))
        k = step * 2 + (0 if lo else 1)
        axis = 0 if step < 2 else 1
        return remote(ref, ref, ss.at[r, part, k], rs.at[r, part, k],
                      device(part, axis, (u if axis == 0 else v) + sign))

    def scatter(part, step, sign, r):
        u, v = coords(part)
        lo = sign > 0
        side = 0 if lo else 1
        if step == 0:
            src = at_part(pa, r, part, LOW if lo else HIGH, wrap(v + 2, 4))
        elif step == 1:
            src = at_part(pa, r, part, ALL, wrap(v + sign, 4))
        elif step == 2:
            src = at_part(pa, r, part, wrap(u + 2, 4), v, side)
        else:
            src = at_part(pa, r, part, wrap(u + sign, 4), v)
        k = 8 + step * 2 + side
        axis = 1 if step < 2 else 0
        return remote(src, land[part][step].at[r, side], ss.at[r, part, k], rs.at[r, part, k],
                      device(part, axis, (u if axis == 0 else v) + sign))

    def block_of(r, core, b):
        return lax.rem(x + r, 4) * 4 + b * 2 + core

    def arrive(r):
        for core in (0, 1):
            for b in (0, 1):
                src = block_of(r, core, b)

                @pl.when(src != me)
                def _():
                    remote(disp_recv.at[src], disp_recv.at[src], disp_ss.at[0], disp_rs.at[src],
                           (src, place)).wait_recv()
            one, two = disp_recv[block_of(r, core, 0)], disp_recv[block_of(r, core, 1)]
            lanes = slice(core * 128, core * 128 + 128)
            xa[r, z, y, 0:HA, lanes] = jnp.concatenate([one[:, :64], two[:, :64]], axis=1)
            xa[r, z, y, HA:RA, lanes] = jnp.concatenate([one[:, 64:], two[:, 64:]], axis=1)

    def units(r):
        for part in range(len(PARTS)):
            for sign in (1, -1):
                gather(part, 3, sign, r, True).wait_recv()
        wait_slots(r)
        rows = xa[r].reshape(16 * RA, COLS)
        more = jnp.concatenate([xc[r, 0].reshape(16 * RC, 128), xc[r, 1].reshape(16 * RC, 128)], axis=1)

        @pl.loop(0, 2)
        def _(i):
            m = pl.ds(pl.multiple_of(i * 256, 256), 256)

            def product(w):
                return jnp.dot(w[m, 0:16 * RA], rows, preferred_element_type=F32) + jnp.dot(
                    w[m, 16 * RA:], more, preferred_element_type=F32)

            gate, up = product(gate_t), product(up_t)
            hidden[m, :] = (gate / (1.0 + jnp.exp(-gate)) * up).astype(BF16)

    def results_c(r):
        @pl.loop(0, 2)
        def _(i):
            m = pl.ds(pl.multiple_of(16 * RA + i * 8 * RC, 128), 8 * RC)
            part = jnp.dot(down_t[m, :], hidden[...], preferred_element_type=F32).astype(BF16)
            s = pl.ds(i * 8, 8)
            pc[r, 0, s] = part[:, :128].reshape(8, RC, 128)
            pc[r, 1, s] = part[:, 128:].reshape(8, RC, 128)

        if r == 0:
            keep(False).start()
            x_back(0, 1 - c).start()
        else:
            for core in (0, 1):
                x_back(r, core).start()

    def results_a(r):
        @pl.loop(0, 4)
        def _(i):
            m = pl.ds(pl.multiple_of(i * 4 * RA, 128), 4 * RA)
            part = jnp.dot(down_t[m, :], hidden[...], preferred_element_type=F32)
            pa[r, i] = part.astype(BF16).reshape(4, RA, COLS)

        for part in range(len(PARTS)):
            for sign in (1, -1):
                scatter(part, 0, sign, r).start()

    def returning(r, core, b):
        target = block_of(r, core, b)
        return remote(ret_send.at[r, core, b], ret_recv.at[me], ret_ss.at[r, core, b], ret_rs.at[me], (target, place))

    def give_back(r):
        rows = []
        for part, (r0, n) in enumerate(PARTS):
            last = land[part][3]
            total = pa[r, z, y, r0:r0 + n].astype(F32) + last[r, 0].astype(F32) + last[r, 1].astype(F32)
            rows.append(total.astype(BF16))
        whole = jnp.concatenate(rows, axis=0)
        for core in (0, 1):
            tile = whole[:, core * 128:core * 128 + 128]
            for b in (0, 1):
                lanes = slice(b * 64, b * 64 + 64)
                ret_send[r, core, b] = jnp.concatenate([tile[0:HA, lanes], tile[HA:RA, lanes]], axis=1)

                @pl.when(block_of(r, core, b) != me)
                def _():
                    returning(r, core, b).start()

                @pl.when(block_of(r, core, b) == me)
                def _():
                    ret_recv[pl.ds(me, 1)] = ret_send[r, core, pl.ds(b, 1)]

    def gather_op(step, r, part):
        if step == 0:
            if ("here", r) not in seen:
                seen.add(("here", r))
                arrive(r)
        else:
            for sign in (1, -1):
                gather(part, step - 1, sign, r, True).wait_recv()
        for sign in (1, -1):
            gather(part, step, sign, r).start()

    def scatter_op(step, r, part):
        for sign in (1, -1):
            scatter(part, step - 1, sign, r).wait_recv()
        if step == 4:
            seen.add(("summed", r, part))
            if all(("summed", r, p) in seen for p in range(len(PARTS))):
                give_back(r)
            return
        u, v = coords(part)
        got = land[part][step - 1]
        if step == 1:
            add_into(at_part(pa, r, part, LOW, wrap(v + 1, 4)), got.at[r, 0])
            add_into(at_part(pa, r, part, HIGH, wrap(v - 1, 4)), got.at[r, 1])
        elif step == 2:
            add_into(at_part(pa, r, part, ALL, v), got.at[r, 0], got.at[r, 1])
        else:
            add_into(at_part(pa, r, part, wrap(u + 1, 4), v, 0), got.at[r, 0])
            add_into(at_part(pa, r, part, wrap(u - 1, 4), v, 1), got.at[r, 1])
        for sign in (1, -1):
            scatter(part, step, sign, r).start()

    def prepare(i):
        m = pl.ds(pl.multiple_of(i * 768, 128), 768)
        wide = pl.ds(pl.multiple_of(i * 4 * RA, 128), 4 * RA)
        thin = pl.ds(pl.multiple_of(16 * RA + i * 4 * RC, 128), 4 * RC)

        def sorted_rows(w):
            return (jnp.concatenate([w[n * 192:n * 192 + RA] for n in range(4)], axis=0),
                    jnp.concatenate([w[n * 192 + RA:n * 192 + 192] for n in range(4)], axis=0))

        for src, dst in ((gate_raw, gate_t), (up_raw, up_t)):
            first, second = sorted_rows(src[m, :])
            dst[:, wide] = first.T
            dst[:, thin] = second.T
        first, second = sorted_rows(down_raw[:, m].T)
        down_t[wide, :] = first
        down_t[thin, :] = second

    def gather_sent():
        swap_meta().wait_send()
        for sign in (1, -1):
            for step in range(6):
                head(step, sign).wait_send()
        x_out(0, 1 - c).wait_send()
        for r in (1, 2, 3):
            for core in (0, 1):
                x_out(r, core).wait_send()
        for d in range(1, 16):
            dispatch(d).wait_send()
        for r in range(GROUPS):
            for part in range(len(PARTS)):
                for sign in (1, -1):
                    for step in range(4):
                        gather(part, step, sign, r).wait_send()

    def sums_sent():
        for sign in (1, -1):
            for step in range(5):
                tail(step, sign).wait_send()
        x_back(0, 1 - c).wait_send()
        for r in (1, 2, 3):
            for core in (0, 1):
                x_back(r, core).wait_send()
        for r in range(GROUPS):
            for part in range(len(PARTS)):
                for sign in (1, -1):
                    for step in range(4):
                        scatter(part, step, sign, r).wait_send()

    seen = set()

    def loaded():
        if "loaded" not in seen:
            seen.add("loaded")
            for load in loads:
                load.wait()

    for op, *at in ORDER:
        if op == "h":
            head_step(*at)
        elif op == "pk":
            if "tokens" not in seen:
                seen.add("tokens")
                for sign in (1, -1):
                    head(5, sign, True).wait_recv()
            pick_slots(*at)
        elif op == "g":
            gather_op(*at)
        elif op == "mu":
            units(*at)
        elif op == "mc":
            results_c(*at)
        elif op == "ma":
            results_a(*at)
        elif op == "s":
            scatter_op(*at)
        elif op == "add":
            added = sum(1 for k in seen if k[0] == "add")
            seen.add(("add", *at))
            add_up(*at, added == 0, added == 3)
        elif op == "t":
            tail_step(*at)
            if at[0] == 2:
                gather_sent()
        elif op == "prep":
            loaded()
            prepare(at[0])
        elif op == "tab":
            tables()
        elif op == "own":
            own_weights()

    sums_sent()
    for d in range(1, 16):
        src = wrap(me + d, 16)
        remote(ret_recv.at[src], ret_recv.at[src], disp_ss.at[0], ret_rs.at[src], (src, place)).wait_recv()
    back = jnp.concatenate([ret_recv[e] for e in range(16)], axis=1)
    mixed = jnp.dot(back, w_high[...], preferred_element_type=F32) + jnp.dot(
        back, w_low[...], preferred_element_type=F32)
    out_ref[0:HA, :] = mixed[:, 0:256].astype(BF16)
    out_ref[HA:RA, :] = mixed[:, 256:512].astype(BF16)

    for sign in (1, -1):
        tail(5, sign).wait_recv()
    out_ref[RA:, :] = (tsum[z8, y].astype(F32) + y2[0].astype(F32) + y2[1].astype(F32)).astype(BF16)

    for sign in (1, -1):
        tail(5, sign).wait_send()
    for r in range(GROUPS):
        for core in (0, 1):
            for b in (0, 1):
                @pl.when(block_of(r, core, b) != me)
                def _():
                    returning(r, core, b).wait_send()


def body(tokens, expert_ids, pair_logits, gate_weight, up_weight, down_weight):
    vmem = pl.BlockSpec(memory_space=pltpu.VMEM)
    hbm = pl.BlockSpec(memory_space=pl.ANY)
    dma = pltpu.SemaphoreType.DMA

    def buf(*shape):
        return pltpu.VMEM(shape, BF16)

    def buf32(*shape):
        return pltpu.VMEM(shape, F32)

    landing = []
    for _, n in PARTS:
        half = (n // 2, COLS) if n % 32 == 0 else (n, 128)
        landing += [
            buf(GROUPS, 2, 2, n, COLS), buf(GROUPS, 2, 4, n, COLS), buf(GROUPS, 2, *half), buf(GROUPS, 2, n, COLS)]
    out = pl.pallas_call(
        kernel,
        out_shape=jax.ShapeDtypeStruct((192, 256), BF16),
        in_specs=[vmem, vmem, vmem, hbm, hbm, hbm],
        out_specs=vmem,
        scratch_shapes=[
            buf(3072, 512), buf(3072, 512), buf(512, 3072),
            buf(512, 3072), buf(512, 3072), buf(3072, 512),
            buf(GROUPS, 4, 4, RA, COLS), buf(GROUPS, 4, 4, RA, COLS), buf(512, COLS),
            buf(2048, 512), buf(2048, 512), buf(2048, 512),
            buf(16, HA, 128), buf(16, HA, 128), buf(GROUPS, 2, 2, HA, 128), buf(16, HA, 128),
            *landing,
            buf32(2, 8, 256), buf32(2, 16, 256), buf32(2, 16, 256),
            buf(1024, 512), buf(1024, 512), buf(1024, 512),
            buf(8, 4, RC, 256), buf(4, 2, 16, RC, 128), buf(4, 2, 16, RC, 128),
            buf(4, 2, 16, RC, 128), buf(4, 2, 16, RC, 128),
            buf32(4, 4 * RC, 512), buf(8, 4, RC, 256),
            buf(2, 2, RC, 256), buf(2, 4, RC, 256), buf(2, 4, RC, 256), buf(2, 4, RC, 256),
            buf(2, HC, 256), buf(2, RC, 256),
            dma((3,)), dma((16,)), dma((16,)), dma((GROUPS, 2, 2)), dma((16,)),
            dma((GROUPS, len(PARTS), 16)), dma((GROUPS, len(PARTS), 16)), dma((25,)), dma((25,)),
            dma((4, 2)), dma((4, 2)), dma((4, 2)), dma((4, 2)), dma((2,)),
        ],
        compiler_params=pltpu.CompilerParams(
            collective_id=0, has_side_effects=True, vmem_limit_bytes=60 * 2**20),
        cost_estimate=pl.CostEstimate(flops=9_700_000_000, bytes_accessed=10_000_000, transcendentals=524288),
    )(tokens.T, expert_ids.T, pair_logits.T, gate_weight[0], up_weight[0], down_weight[0])
    return out.T


def solution(mesh):
    in_specs = (
        P("expert", "split"),
        P("expert", None),
        P("expert", None),
        P("expert", None, "split"),
        P("expert", None, "split"),
        P("expert", "split", None),
    )
    return jax.shard_map(body, mesh=mesh, in_specs=in_specs, out_specs=P("expert", "split"), check_vma=False)
```

```python
import functools

import jax
import jax.numpy as jnp
from jax import lax
from jax.experimental import pallas as pl
from jax.experimental.pallas import tpu as pltpu
from jax.sharding import PartitionSpec as P

MESH = pl.DeviceIdType.MESH
BF16 = jnp.bfloat16
F32 = jnp.float32

COLS = 256
GROUPS = 4
PARTS = ((0, 128), (128, 32))
RA = 160
RC = 32
HA, HC = RA // 2, RC // 2
ORDER = (
    ("h", 1), ("g", 0, 0, 0), ("g", 0, 1, 1), ("g", 0, 3, 0), ("g", 1, 0, 0), ("tab",),
    ("g", 0, 2, 1), ("h", 2), ("g", 1, 3, 0), ("prep", 2), ("g", 0, 0, 1), ("g", 1, 2, 1),
    ("g", 0, 1, 0), ("g", 2, 0, 0), ("g", 1, 0, 1), ("h", 3), ("g", 2, 3, 0), ("g", 0, 3, 1),
    ("g", 0, 2, 0), ("g", 1, 1, 0), ("h", 4), ("g", 1, 1, 1), ("g", 2, 0, 1), ("g", 3, 0, 0),
    ("h", 5), ("g", 2, 1, 0), ("g", 1, 2, 0), ("g", 2, 2, 1), ("pk", 1), ("g", 1, 3, 1),
    ("prep", 1), ("pk", 3), ("g", 3, 0, 1), ("g", 2, 2, 0), ("g", 2, 1, 1), ("prep", 3),
    ("pk", 0), ("pk", 2), ("g", 3, 1, 0), ("prep", 0), ("g", 2, 3, 1), ("mu", 0),
    ("g", 3, 1, 1), ("g", 3, 3, 0), ("mc", 0), ("g", 3, 3, 1), ("ma", 0), ("g", 3, 2, 0),
    ("mu", 1), ("g", 3, 2, 1), ("mc", 1), ("ma", 1), ("mu", 3), ("s", 1, 0, 1),
    ("mc", 3), ("ma", 3), ("s", 1, 0, 0), ("mu", 2), ("s", 1, 1, 1), ("mc", 2),
    ("s", 1, 3, 1), ("ma", 2), ("s", 1, 1, 0), ("add", 0), ("add", 1), ("add", 3),
    ("s", 2, 0, 0), ("add", 2), ("s", 1, 2, 1), ("s", 2, 0, 1), ("s", 1, 3, 0), ("t", 0),
    ("s", 2, 3, 1), ("s", 3, 0, 0), ("s", 2, 1, 1), ("t", 1), ("s", 2, 1, 0), ("s", 2, 2, 1),
    ("s", 1, 2, 0), ("t", 2), ("s", 2, 3, 0), ("s", 3, 1, 0), ("s", 3, 3, 1), ("s", 3, 2, 1),
    ("s", 2, 2, 0), ("s", 3, 3, 0), ("s", 4, 3, 1), ("s", 4, 2, 1), ("s", 4, 0, 0), ("t", 3),
    ("s", 4, 1, 0), ("s", 3, 2, 0), ("s", 3, 1, 1), ("t", 4), ("s", 4, 1, 1), ("s", 4, 3, 0),
    ("s", 3, 0, 1), ("t", 5), ("s", 4, 2, 0), ("s", 4, 0, 1), ("own",),
)
FAR = (0, 1, 3, 2)


def wrap(i, n):
    return lax.rem(i + n, n)


def kernel(
    tok_ref, ids_ref, logit_ref, gate_hbm, up_hbm, down_hbm, out_ref,
    gate_raw, up_raw, down_raw, gate_t, up_t, down_t,
    xa, pa, hidden, sel, w_high, w_low,
    disp_send, disp_recv, ret_send, ret_recv, a1, a2, a3, a4, b1, b2, b3, b4,
    meta, slots, mixes, sel_c, wc_high, wc_low,
    raw, xs, xc, pc, tr, acc, tsum, z1, z2, z3, z4, y1, y2,
    weight_sem, disp_ss, disp_rs, ret_ss, ret_rs, ss, rs, cs, cr, xss, xrs, tss, trs, local_sem,
):
    me = lax.axis_index("expert")
    place = lax.axis_index("split")
    x = me // 4
    zl = lax.rem(me // 2, 2)
    c = lax.rem(me, 2)
    z = place // 4
    y = lax.rem(place, 4)
    z8 = z * 2 + zl

    def at_z(zz):
        return (me, wrap(zz, 4) * 4 + y)

    def at_y(yy):
        return (me, z * 4 + wrap(yy, 4))

    def at_z8(zz):
        w = wrap(zz, 8)
        return (x * 4 + lax.rem(w, 2) * 2 + c, (w // 2) * 4 + y)

    def at_x(r, core):
        return (lax.rem(x + r, 4) * 4 + zl * 2 + core, place)

    def remote(src, dst, send, recv, dev):
        return pltpu.make_async_remote_copy(
            src_ref=src, dst_ref=dst, send_sem=send, recv_sem=recv, device_id=dev, device_id_type=MESH)

    barrier = pltpu.get_barrier_semaphore()
    for d in range(1, 16):
        pl.semaphore_signal(barrier, inc=1, device_id=(wrap(me + d, 16), place), device_id_type=MESH)
    for dev in (at_z(z + 1), at_z(z - 1), at_y(y + 1), at_y(y - 1), at_z8(z8 + 2 * zl - 1)):
        pl.semaphore_signal(barrier, inc=1, device_id=dev, device_id_type=MESH)

    loads = [
        pltpu.make_async_copy(src, dst, weight_sem.at[i])
        for i, (src, dst) in enumerate(((gate_hbm, gate_raw), (up_hbm, up_raw), (down_hbm, down_raw)))
    ]
    for load in loads:
        load.start()

    tok = tok_ref[...]
    raw[z8, y] = tok[RA:, :]
    meta[zl, 0:2, :] = ids_ref[...].astype(F32)
    meta[zl, 2:4, :] = logit_ref[...]
    meta[zl, 4:8, :] = jnp.zeros((4, 256), F32)

    def swap_meta():
        return remote(meta.at[zl], meta.at[zl], cs.at[24], cr.at[24], (x * 4 + (1 - zl) * 2 + c, place))

    def head(step, sign, arriving=False):
        lo = sign > 0
        k = step * 2 + (0 if lo else 1)
        back = -sign if arriving else 0
        if step == 0:
            ref = raw.at[z8, wrap(y + back, 4)]
        elif step == 1:
            ref = raw.at[z8, wrap(y - sign + back + 4, 4), pl.ds(0 if lo else HC, HC)]
        else:
            n = step - 2
            chunk = wrap(z8 - sign * n + back + 8, 8)
            ref = raw.at[chunk] if n < 3 else raw.at[chunk, pl.ds(0 if lo else 2, 2)]
        return remote(ref, ref, cs.at[k], cr.at[k], at_y(y + sign) if step < 2 else at_z8(z8 + sign))

    def head_step(step):
        for sign in (1, -1):
            head(step - 1, sign, True).wait_recv()
        for sign in (1, -1):
            head(step, sign).start()

    labels = lax.broadcasted_iota(jnp.int32, (16, 256), 0).astype(F32)
    earlier = lax.broadcasted_iota(jnp.int32, (256, 256), 0) < lax.broadcasted_iota(jnp.int32, (256, 256), 1)
    earlier = jnp.where(earlier, 1.0, 0.0).astype(BF16)
    sub = lax.broadcasted_iota(jnp.int32, (64, 256), 0).astype(F32)
    zero = jnp.zeros((64, 256), BF16)

    def slot_of(ids):
        hits = jnp.where((ids[0:1, :] == labels) | (ids[1:2, :] == labels), 1.0, 0.0)
        count = jnp.dot(hits.astype(BF16), earlier, preferred_element_type=F32)
        return jnp.where(hits > 0.5, count, -1.0)

    def mix_of(ids, logits):
        first = 1.0 / (1.0 + jnp.exp(logits[1:2, :] - logits[0:1, :]))
        return jnp.where(ids[0:1, :] == labels, first, jnp.where(ids[1:2, :] == labels, 1.0 - first, 0.0))

    ids = ids_ref[...].astype(F32)
    slot = slot_of(ids)
    mix = mix_of(ids, logit_ref[...])

    def one_hot(row):
        return jnp.where(sub == row, 1.0, 0.0).astype(BF16)

    def split(row, w):
        full = jnp.where(sub == row, w, 0.0)
        top = full.astype(BF16)
        return top, (full - top.astype(F32)).astype(BF16)

    def place_two(ref, base, first, second):
        ref[base:base + 64, 0:256] = first
        ref[base:base + 64, 256:512] = zero
        ref[base + 64:base + 128, 0:256] = zero
        ref[base + 64:base + 128, 256:512] = second

    for e in range(16):
        one = one_hot(slot[e:e + 1, :])
        place_two(sel, e * 128, one, one)

    pl.semaphore_wait(barrier, 20)
    swap_meta().start()
    for sign in (1, -1):
        head(0, sign).start()

    halves = jnp.concatenate([tok[0:HA, :], tok[HA:RA, :]], axis=1)
    for e in range(16):
        disp_send[e] = lax.dot_general(
            halves, sel[e * 128:e * 128 + 128, :], (((1,), (1,)), ((), ())), preferred_element_type=F32
        ).astype(BF16)
    disp_recv[pl.ds(me, 1)] = disp_send[pl.ds(me, 1)]

    def dispatch(d):
        step, inner = d // 4, d % 4
        target = wrap(x + FAR[step], 4) * 4 + wrap(me - x * 4 + inner, 4)
        return remote(disp_send.at[target], disp_recv.at[me], disp_ss.at[d], disp_rs.at[me], (target, place))

    for d in range(1, 16):
        dispatch(d).start()

    def tables():
        remote(meta.at[zl], meta.at[1 - zl], cs.at[24], cr.at[24], (x * 4 + (1 - zl) * 2 + c, place)).wait_recv()
        for b in (0, 1):
            both = meta[b]
            slots[b] = slot_of(both[0:2])
            mixes[b] = mix_of(both[0:2], both[2:4])
        for r in range(4):
            for core in (0, 1):
                e = lax.rem(x + r, 4) * 4 + zl * 2 + core
                base = r * 256 + core * 128
                row = [slots[b, pl.ds(e, 1), :] for b in (0, 1)]
                w = [mixes[b, pl.ds(e, 1), :] for b in (0, 1)]
                place_two(sel_c, base, one_hot(row[0]), one_hot(row[1]))
                first, second = split(row[0], w[0]), split(row[1], w[1])
                place_two(wc_high, base, first[0], second[0])
                place_two(wc_low, base, first[1], second[1])

    def own_weights():
        for e in range(16):
            top, rest = split(slot[e:e + 1, :], mix[e:e + 1, :])
            place_two(w_high, e * 128, top, top)
            place_two(w_low, e * 128, rest, rest)

    def x_out(r, core):
        return remote(xs.at[r, core], xc.at[(4 - r) % 4, c], xss.at[r, core], xrs.at[(4 - r) % 4, c], at_x(r, core))

    def x_back(r, core):
        return remote(pc.at[r, core], tr.at[(4 - r) % 4, c], tss.at[r, core], trs.at[(4 - r) % 4, c], at_x(r, core))

    def keep(out):
        src, dst, i = (xs.at[0, c], xc.at[0, c], 0) if out else (pc.at[0, c], tr.at[0, c], 1)
        return pltpu.make_async_copy(src, dst, local_sem.at[i])

    def x_arrived(refs, sems, r, core):
        remote(refs.at[r, core], refs.at[r, core], xss.at[0, 0], sems.at[r, core], at_x(r, core)).wait_recv()

    def pick_slots(r):
        base = r * 256

        @pl.loop(0, 4)
        def _(i):
            first = raw[i * 2].reshape(4 * RC, 256)
            second = raw[i * 2 + 1].reshape(4 * RC, 256)
            got = lax.dot_general(
                first, sel_c[base:base + 256, 0:256], (((1,), (1,)), ((), ())), preferred_element_type=F32)
            got = got + lax.dot_general(
                second, sel_c[base:base + 256, 256:512], (((1,), (1,)), ((), ())), preferred_element_type=F32)
            got = got.astype(BF16)
            s = pl.ds(i * 4, 4)
            xs[r, 0, s] = got[:, :128].reshape(4, RC, 128)
            xs[r, 1, s] = got[:, 128:].reshape(4, RC, 128)

        if r == 0:
            keep(True).start()
            x_out(0, 1 - c).start()
        else:
            for core in (0, 1):
                x_out(r, core).start()

    def wait_slots(r):
        if r == 0:
            keep(True).wait()
            x_arrived(xc, xrs, 0, 1 - c)
        else:
            for core in (0, 1):
                x_arrived(xc, xrs, r, core)

    def add_up(r, first, last):
        if r == 0:
            keep(False).wait()
            x_arrived(tr, trs, 0, 1 - c)
        else:
            for core in (0, 1):
                x_arrived(tr, trs, r, core)

        @pl.loop(0, 4)
        def _(i):
            s = pl.ds(i * 4, 4)
            rows = jnp.concatenate(
                [tr[r, 0, s].reshape(4 * RC, 128), tr[r, 1, s].reshape(4 * RC, 128)], axis=1)
            base = r * 256
            total = jnp.dot(rows, wc_high[base:base + 256, :], preferred_element_type=F32)
            total = total + jnp.dot(rows, wc_low[base:base + 256, :], preferred_element_type=F32)
            if not first:
                total = total + acc[i]
            if last:
                total = total.astype(BF16)
                tsum[i * 2] = total[:, 0:256].reshape(4, RC, 256)
                tsum[i * 2 + 1] = total[:, 256:512].reshape(4, RC, 256)
            else:
                acc[i] = total

    def add_into(ref, *others):
        total = ref[...].astype(F32)
        for o in others:
            total = total + o[...].astype(F32)
        ref[...] = total.astype(BF16)

    tail_land = (z1, z2, z3, z4, y1, y2)

    def tail(step, sign):
        lo = sign > 0
        side = 0 if lo else 1
        k = 12 + step * 2 + side
        if step == 0:
            src = tsum.at[wrap(z8 + 4, 8), pl.ds(0 if lo else 2, 2)]
        elif step < 4:
            src = tsum.at[wrap(z8 + sign * (4 - step), 8)]
        elif step == 4:
            src = tsum.at[z8, wrap(y + 2, 4), pl.ds(0 if lo else HC, HC)]
        else:
            src = tsum.at[z8, wrap(y + sign, 4)]
        return remote(src, tail_land[step].at[side], cs.at[k], cr.at[k],
                      at_z8(z8 + sign) if step < 4 else at_y(y + sign))

    def tail_step(step):
        if step > 0:
            for sign in (1, -1):
                tail(step - 1, sign).wait_recv()
        got = tail_land[step - 1]
        if step == 1:
            add_into(tsum.at[wrap(z8 + 3, 8), pl.ds(0, 2)], got.at[0])
            add_into(tsum.at[wrap(z8 - 3, 8), pl.ds(2, 2)], got.at[1])
        elif step in (2, 3):
            add_into(tsum.at[wrap(z8 + 4 - step, 8)], got.at[0])
            add_into(tsum.at[wrap(z8 - 4 + step, 8)], got.at[1])
        elif step == 4:
            add_into(tsum.at[z8], got.at[0], got.at[1])
        elif step == 5:
            add_into(tsum.at[z8, wrap(y + 1, 4), pl.ds(0, HC)], got.at[0])
            add_into(tsum.at[z8, wrap(y - 1, 4), pl.ds(HC, HC)], got.at[1])
        for sign in (1, -1):
            tail(step, sign).start()

    land = ((a1, a2, a3, a4), (b1, b2, b3, b4))

    def at_part(ref, r, part, i, j, half=None):
        r0, n = PARTS[part]
        zi, yi = (i, j) if part == 0 else (j, i)
        if half is None:
            return ref.at[r, zi, yi, pl.ds(r0, n)]
        if n % 32 == 0:
            return ref.at[r, zi, yi, pl.ds(r0 + half * (n // 2), n // 2)]
        return ref.at[r, zi, yi, pl.ds(r0, n), pl.ds(half * 128, 128)]

    def coords(part):
        return (z, y) if part == 0 else (y, z)

    def device(part, axis, i):
        return at_z(i) if axis == part else at_y(i)

    ALL, LOW, HIGH = pl.ds(0, 4), pl.ds(0, 2), pl.ds(2, 2)

    def gather(part, step, sign, r, arriving=False):
        u, v = coords(part)
        back = -sign if arriving else 0
        lo = sign > 0
        if step == 0:
            ref = at_part(xa, r, part, wrap(u + back, 4), v)
        elif step == 1:
            ref = at_part(xa, r, part, wrap(u - sign + back + 4, 4), v, 0 if lo else 1)
        elif step == 2:
            ref = at_part(xa, r, part, ALL, wrap(v + back, 4))
        else:
            ref = at_part(xa, r, part, LOW if lo else HIGH, wrap(v - sign + back + 4, 4))
        k = step * 2 + (0 if lo else 1)
        axis = 0 if step < 2 else 1
        return remote(ref, ref, ss.at[r, part, k], rs.at[r, part, k],
                      device(part, axis, (u if axis == 0 else v) + sign))

    def scatter(part, step, sign, r):
        u, v = coords(part)
        lo = sign > 0
        side = 0 if lo else 1
        if step == 0:
            src = at_part(pa, r, part, LOW if lo else HIGH, wrap(v + 2, 4))
        elif step == 1:
            src = at_part(pa, r, part, ALL, wrap(v + sign, 4))
        elif step == 2:
            src = at_part(pa, r, part, wrap(u + 2, 4), v, side)
        else:
            src = at_part(pa, r, part, wrap(u + sign, 4), v)
        k = 8 + step * 2 + side
        axis = 1 if step < 2 else 0
        return remote(src, land[part][step].at[r, side], ss.at[r, part, k], rs.at[r, part, k],
                      device(part, axis, (u if axis == 0 else v) + sign))

    def block_of(r, core, b):
        return lax.rem(x + r, 4) * 4 + b * 2 + core

    def arrive(r):
        for core in (0, 1):
            for b in (0, 1):
                src = block_of(r, core, b)

                @pl.when(src != me)
                def _():
                    remote(disp_recv.at[src], disp_recv.at[src], disp_ss.at[0], disp_rs.at[src],
                           (src, place)).wait_recv()
            one, two = disp_recv[block_of(r, core, 0)], disp_recv[block_of(r, core, 1)]
            lanes = slice(core * 128, core * 128 + 128)
            xa[r, z, y, 0:HA, lanes] = jnp.concatenate([one[:, :64], two[:, :64]], axis=1)
            xa[r, z, y, HA:RA, lanes] = jnp.concatenate([one[:, 64:], two[:, 64:]], axis=1)

    def units(r):
        for part in range(len(PARTS)):
            for sign in (1, -1):
                gather(part, 3, sign, r, True).wait_recv()
        wait_slots(r)
        rows = xa[r].reshape(16 * RA, COLS)
        more = jnp.concatenate([xc[r, 0].reshape(16 * RC, 128), xc[r, 1].reshape(16 * RC, 128)], axis=1)

        @pl.loop(0, 2)
        def _(i):
            m = pl.ds(pl.multiple_of(i * 256, 256), 256)

            def product(w):
                return jnp.dot(w[m, 0:16 * RA], rows, preferred_element_type=F32) + jnp.dot(
                    w[m, 16 * RA:], more, preferred_element_type=F32)

            gate, up = product(gate_t), product(up_t)
            hidden[m, :] = (gate / (1.0 + jnp.exp(-gate)) * up).astype(BF16)

    def results_c(r):
        @pl.loop(0, 2)
        def _(i):
            m = pl.ds(pl.multiple_of(16 * RA + i * 8 * RC, 128), 8 * RC)
            part = jnp.dot(down_t[m, :], hidden[...], preferred_element_type=F32).astype(BF16)
            s = pl.ds(i * 8, 8)
            pc[r, 0, s] = part[:, :128].reshape(8, RC, 128)
            pc[r, 1, s] = part[:, 128:].reshape(8, RC, 128)

        if r == 0:
            keep(False).start()
            x_back(0, 1 - c).start()
        else:
            for core in (0, 1):
                x_back(r, core).start()

    def results_a(r):
        @pl.loop(0, 4)
        def _(i):
            m = pl.ds(pl.multiple_of(i * 4 * RA, 128), 4 * RA)
            part = jnp.dot(down_t[m, :], hidden[...], preferred_element_type=F32)
            pa[r, i] = part.astype(BF16).reshape(4, RA, COLS)

        for part in range(len(PARTS)):
            for sign in (1, -1):
                scatter(part, 0, sign, r).start()

    def returning(r, core, b):
        target = block_of(r, core, b)
        return remote(ret_send.at[r, core, b], ret_recv.at[me], ret_ss.at[r, core, b], ret_rs.at[me], (target, place))

    def give_back(r):
        rows = []
        for part, (r0, n) in enumerate(PARTS):
            last = land[part][3]
            total = pa[r, z, y, r0:r0 + n].astype(F32) + last[r, 0].astype(F32) + last[r, 1].astype(F32)
            rows.append(total.astype(BF16))
        whole = jnp.concatenate(rows, axis=0)
        for core in (0, 1):
            tile = whole[:, core * 128:core * 128 + 128]
            for b in (0, 1):
                lanes = slice(b * 64, b * 64 + 64)
                ret_send[r, core, b] = jnp.concatenate([tile[0:HA, lanes], tile[HA:RA, lanes]], axis=1)

                @pl.when(block_of(r, core, b) != me)
                def _():
                    returning(r, core, b).start()

                @pl.when(block_of(r, core, b) == me)
                def _():
                    ret_recv[pl.ds(me, 1)] = ret_send[r, core, pl.ds(b, 1)]

    def gather_op(step, r, part):
        if step == 0:
            if ("here", r) not in seen:
                seen.add(("here", r))
                arrive(r)
        else:
            for sign in (1, -1):
                gather(part, step - 1, sign, r, True).wait_recv()
        for sign in (1, -1):
            gather(part, step, sign, r).start()

    def scatter_op(step, r, part):
        for sign in (1, -1):
            scatter(part, step - 1, sign, r).wait_recv()
        if step == 4:
            seen.add(("summed", r, part))
            if all(("summed", r, p) in seen for p in range(len(PARTS))):
                give_back(r)
            return
        u, v = coords(part)
        got = land[part][step - 1]
        if step == 1:
            add_into(at_part(pa, r, part, LOW, wrap(v + 1, 4)), got.at[r, 0])
            add_into(at_part(pa, r, part, HIGH, wrap(v - 1, 4)), got.at[r, 1])
        elif step == 2:
            add_into(at_part(pa, r, part, ALL, v), got.at[r, 0], got.at[r, 1])
        else:
            add_into(at_part(pa, r, part, wrap(u + 1, 4), v, 0), got.at[r, 0])
            add_into(at_part(pa, r, part, wrap(u - 1, 4), v, 1), got.at[r, 1])
        for sign in (1, -1):
            scatter(part, step, sign, r).start()

    def prepare(i):
        m = pl.ds(pl.multiple_of(i * 768, 128), 768)
        wide = pl.ds(pl.multiple_of(i * 4 * RA, 128), 4 * RA)
        thin = pl.ds(pl.multiple_of(16 * RA + i * 4 * RC, 128), 4 * RC)

        def sorted_rows(w):
            return (jnp.concatenate([w[n * 192:n * 192 + RA] for n in range(4)], axis=0),
                    jnp.concatenate([w[n * 192 + RA:n * 192 + 192] for n in range(4)], axis=0))

        for src, dst in ((gate_raw, gate_t), (up_raw, up_t)):
            first, second = sorted_rows(src[m, :])
            dst[:, wide] = first.T
            dst[:, thin] = second.T
        first, second = sorted_rows(down_raw[:, m].T)
        down_t[wide, :] = first
        down_t[thin, :] = second

    def gather_sent():
        swap_meta().wait_send()
        for sign in (1, -1):
            for step in range(6):
                head(step, sign).wait_send()
        x_out(0, 1 - c).wait_send()
        for r in (1, 2, 3):
            for core in (0, 1):
                x_out(r, core).wait_send()
        for d in range(1, 16):
            dispatch(d).wait_send()
        for r in range(GROUPS):
            for part in range(len(PARTS)):
                for sign in (1, -1):
                    for step in range(4):
                        gather(part, step, sign, r).wait_send()

    def sums_sent():
        for sign in (1, -1):
            for step in range(5):
                tail(step, sign).wait_send()
        x_back(0, 1 - c).wait_send()
        for r in (1, 2, 3):
            for core in (0, 1):
                x_back(r, core).wait_send()
        for r in range(GROUPS):
            for part in range(len(PARTS)):
                for sign in (1, -1):
                    for step in range(4):
                        scatter(part, step, sign, r).wait_send()

    seen = set()

    def loaded():
        if "loaded" not in seen:
            seen.add("loaded")
            for load in loads:
                load.wait()

    for op, *at in ORDER:
        if op == "h":
            head_step(*at)
        elif op == "pk":
            if "tokens" not in seen:
                seen.add("tokens")
                for sign in (1, -1):
                    head(5, sign, True).wait_recv()
            pick_slots(*at)
        elif op == "g":
            gather_op(*at)
        elif op == "mu":
            units(*at)
        elif op == "mc":
            results_c(*at)
        elif op == "ma":
            results_a(*at)
        elif op == "s":
            scatter_op(*at)
        elif op == "add":
            added = sum(1 for k in seen if k[0] == "add")
            seen.add(("add", *at))
            add_up(*at, added == 0, added == 3)
        elif op == "t":
            tail_step(*at)
            if at[0] == 2:
                gather_sent()
        elif op == "prep":
            loaded()
            prepare(at[0])
        elif op == "tab":
            tables()
        elif op == "own":
            own_weights()

    sums_sent()
    for d in range(1, 16):
        src = wrap(me + d, 16)
        remote(ret_recv.at[src], ret_recv.at[src], disp_ss.at[0], ret_rs.at[src], (src, place)).wait_recv()
    back = jnp.concatenate([ret_recv[e] for e in range(16)], axis=1)
    mixed = jnp.dot(back, w_high[...], preferred_element_type=F32) + jnp.dot(
        back, w_low[...], preferred_element_type=F32)
    out_ref[0:HA, :] = mixed[:, 0:256].astype(BF16)
    out_ref[HA:RA, :] = mixed[:, 256:512].astype(BF16)

    for sign in (1, -1):
        tail(5, sign).wait_recv()
    out_ref[RA:, :] = (tsum[z8, y].astype(F32) + y2[0].astype(F32) + y2[1].astype(F32)).astype(BF16)

    for sign in (1, -1):
        tail(5, sign).wait_send()
    for r in range(GROUPS):
        for core in (0, 1):
            for b in (0, 1):
                @pl.when(block_of(r, core, b) != me)
                def _():
                    returning(r, core, b).wait_send()


def body(tokens, expert_ids, pair_logits, gate_weight, up_weight, down_weight):
    vmem = pl.BlockSpec(memory_space=pltpu.VMEM)
    hbm = pl.BlockSpec(memory_space=pl.ANY)
    dma = pltpu.SemaphoreType.DMA

    def buf(*shape):
        return pltpu.VMEM(shape, BF16)

    def buf32(*shape):
        return pltpu.VMEM(shape, F32)

    landing = []
    for _, n in PARTS:
        half = (n // 2, COLS) if n % 32 == 0 else (n, 128)
        landing += [
            buf(GROUPS, 2, 2, n, COLS), buf(GROUPS, 2, 4, n, COLS), buf(GROUPS, 2, *half), buf(GROUPS, 2, n, COLS)]
    out = pl.pallas_call(
        kernel,
        out_shape=jax.ShapeDtypeStruct((192, 256), BF16),
        in_specs=[vmem, vmem, vmem, hbm, hbm, hbm],
        out_specs=vmem,
        scratch_shapes=[
            buf(3072, 512), buf(3072, 512), buf(512, 3072),
            buf(512, 3072), buf(512, 3072), buf(3072, 512),
            buf(GROUPS, 4, 4, RA, COLS), buf(GROUPS, 4, 4, RA, COLS), buf(512, COLS),
            buf(2048, 512), buf(2048, 512), buf(2048, 512),
            buf(16, HA, 128), buf(16, HA, 128), buf(GROUPS, 2, 2, HA, 128), buf(16, HA, 128),
            *landing,
            buf32(2, 8, 256), buf32(2, 16, 256), buf32(2, 16, 256),
            buf(1024, 512), buf(1024, 512), buf(1024, 512),
            buf(8, 4, RC, 256), buf(4, 2, 16, RC, 128), buf(4, 2, 16, RC, 128),
            buf(4, 2, 16, RC, 128), buf(4, 2, 16, RC, 128),
            buf32(4, 4 * RC, 512), buf(8, 4, RC, 256),
            buf(2, 2, RC, 256), buf(2, 4, RC, 256), buf(2, 4, RC, 256), buf(2, 4, RC, 256),
            buf(2, HC, 256), buf(2, RC, 256),
            dma((3,)), dma((16,)), dma((16,)), dma((GROUPS, 2, 2)), dma((16,)),
            dma((GROUPS, len(PARTS), 16)), dma((GROUPS, len(PARTS), 16)), dma((25,)), dma((25,)),
            dma((4, 2)), dma((4, 2)), dma((4, 2)), dma((4, 2)), dma((2,)),
        ],
        compiler_params=pltpu.CompilerParams(
            collective_id=0, has_side_effects=True, vmem_limit_bytes=60 * 2**20),
        cost_estimate=pl.CostEstimate(flops=9_700_000_000, bytes_accessed=10_000_000, transcendentals=524288),
    )(tokens.T, expert_ids.T, pair_logits.T, gate_weight[0], up_weight[0], down_weight[0])
    return out.T


def solution(mesh):
    in_specs = (
        P("expert", "split"),
        P("expert", None),
        P("expert", None),
        P("expert", None, "split"),
        P("expert", None, "split"),
        P("expert", "split", None),
    )
    return jax.shard_map(body, mesh=mesh, in_specs=in_specs, out_specs=P("expert", "split"), check_vma=False)
```
